32 devices in a mesh: dp: 8 (over z, x), expert: 4 (over y, core).
Axes of the slice: x: 2, y: 2, z: 4, core: 2. Of those that a mesh axis runs over, the one named last changes fastest.
Arguments:
- grad: bfloat16 [16, 7168, 2048], P('expert', 'dp')
- momentum: float32 [16, 7168, 2048], P('expert', 'dp'), may hold values from -6 to 6
- placement: int32 [16], replicated, may hold values from 0 to 15, as said below
Outputs:
- momentum_new: float32 [16, 7168, 2048], P('expert', 'dp')
- update: bfloat16 [16, 7168, 2048], P('expert', 'dp')
The draws below stay inside these ranges and needn't reach their ends.
Inputs may be any that keep to these rules, and one draw needn't show every extreme that they name: placement is a permutation; position e lies in group e // 4, and placement[e] // 4 is the new group. The 4 experts of each group go to 4 different groups, so every group receives exactly one expert from every group.
All inputs are finite; a program needn't handle non-finite values.
Results may differ from the reference program's by a relative error of at most 0.0074.
Values may be sent and summed in bfloat16 or wider, within the bound.
No kernel may reach another device: no remote copies, remote signals or barrier semaphores. Data moves between devices by JAX's collectives and lax.ppermute only.
A program may use at most 192 MiB of HBM per device.

```python
import math
import jax
import jax.numpy as jnp
from jax import lax

D = 7168
FF = 2048
LOCAL = 4
EXPERTS = 16


def draw_grad(key, part):
    key = jax.random.fold_in(key, 11)
    key_base, key_rows, key_cols = jax.random.split(key, 3)
    base = jnp.clip(jax.random.normal(key_base, (EXPERTS, D, FF), jnp.float32), -6.0, 6.0)
    row_scale = jnp.exp(jax.random.uniform(key_rows, (EXPERTS, D, 1), jnp.float32, 0.0, math.log(10.0)))
    col_scale = jnp.exp(jax.random.uniform(key_cols, (EXPERTS, 1, FF), jnp.float32, 0.0, math.log(3.0)))
    return (base * row_scale * col_scale).astype(jnp.bfloat16)


def draw_placement(key, part):
    key = jax.random.fold_in(key, 23)
    key_slot, key_source, key_block = jax.random.split(key, 3)
    perm_slot = jax.random.permutation(key_slot, LOCAL)
    perm_source = jax.random.permutation(key_source, LOCAL)
    perm_block = jax.random.permutation(key_block, LOCAL)
    sources = jnp.arange(LOCAL, dtype=jnp.int32)[:, None]
    slot_ids = jnp.arange(LOCAL, dtype=jnp.int32)[None, :]
    targets = (perm_slot[slot_ids] + perm_source[sources]) % LOCAL
    new_slot = (perm_block[sources] + targets) % LOCAL
    return (targets * LOCAL + new_slot).reshape(-1).astype(jnp.int32)


def level_of(key, extent, cuts, smallest, top_value):
    gain = 1.0
    for dim, shards_of in cuts:
        heights = jax.random.uniform(jax.random.fold_in(jax.random.fold_in(key, 6), dim), (shards_of,), jnp.float32, smallest / len(cuts), top_value / len(cuts))
        gain = gain * jnp.repeat(jnp.exp(heights), extent[dim] // shards_of).reshape((-1,) + (1,) * (len(extent) - 1 - dim))
    return gain


def normal_values(own_key, extent, spread, reach, pieces=(), kind=jnp.bfloat16):
    loudness = level_of(own_key, extent, pieces, -0.22, 0.18) if pieces else 1.0
    entries = jax.random.normal(own_key, extent, jnp.float32) * spread * loudness
    return jnp.minimum(jnp.maximum(entries, -reach), reach).astype(kind)


def setup_inputs(seed: int = 0) -> dict:
    keys = jax.random.split(jax.random.key(seed), 4)
    grad = draw_grad(jax.random.fold_in(keys[3], 71), 0)
    momentum = normal_values(keys[1], (EXPERTS, D, FF), 1.0, 6.0, ((0, 4), (1, 8)), jnp.float32)
    placement = draw_placement(jax.random.fold_in(keys[3], 71), 0)
    return dict(grad=grad, momentum=momentum, placement=placement)


def orthogonalize(moved_one):
    values = moved_one.astype(jnp.float32)
    squares = jnp.sum(values * values)
    factor = 0.5 * math.sqrt(FF) / jnp.sqrt(squares + 1e-06)
    normal = (values * factor).astype(jnp.bfloat16)
    gram_whole = jnp.dot(normal.T, normal, preferred_element_type=jnp.float32).astype(jnp.bfloat16)
    product = jnp.dot(normal, gram_whole, preferred_element_type=jnp.float32).astype(jnp.bfloat16)
    second = jnp.dot(product, gram_whole, preferred_element_type=jnp.float32)
    orthogonal = 3.4445 * normal.astype(jnp.float32) - 4.775 * product.astype(jnp.float32) + 2.0315 * second
    return (orthogonal * math.sqrt(D)).astype(jnp.bfloat16)

def reference(grad, momentum, placement):
    momentum_new = 0.95 * momentum + grad.astype(jnp.float32)
    moved = momentum_new.astype(jnp.bfloat16)
    results = lax.map(orthogonalize, moved)
    update = jnp.zeros_like(results).at[placement.astype(jnp.int32)].set(results)
    return (momentum_new, update)
```

```python
import functools
import math

import jax
import jax.numpy as jnp
from jax import lax
from jax.experimental import pallas as pl
from jax.experimental.pallas import tpu as pltpu
from jax.sharding import PartitionSpec as P

D = 7168
BLOCK = 256
VMEM_BYTES = 56 * 2**20


def row_block(rows, most):
    for size in range(most, 15, -16):
        if rows % size == 0:
            return size
    return rows


def momentum_kernel(order_ref, grad_ref, momentum_ref, *refs):
    new_ref, moved_ref, squares_ref = refs[-3:]
    new = 0.95 * momentum_ref[0] + grad_ref[0].astype(jnp.float32)
    new_ref[0] = new
    moved = new.astype(jnp.bfloat16)
    moved_ref[...] = moved
    values = moved.astype(jnp.float32)
    rows, columns = values.shape
    partial_sum = jnp.sum((values * values).reshape(rows // 8, 8, columns), axis=0)

    @pl.when(pl.program_id(0) == 0)
    def _():
        squares_ref[...] = partial_sum

    @pl.when(pl.program_id(0) > 0)
    def _():
        squares_ref[...] += partial_sum


def momentum_step(source, grad, momentum, earlier):
    local_count, rows, columns = grad.shape
    step = row_block(rows, 128)
    spot = pl.BlockSpec((1, step, columns), lambda r, order: (order[0], r, 0))
    in_specs = [spot, spot]
    operands = [source, grad, momentum]
    aliases = {}
    if earlier is not None:
        in_specs.append(pl.BlockSpec(memory_space=pl.ANY))
        operands.append(earlier)
        aliases = {3: 0}
    return pl.pallas_call(
        momentum_kernel,
        grid_spec=pltpu.PrefetchScalarGridSpec(
            num_scalar_prefetch=1,
            grid=(rows // step,),
            in_specs=in_specs,
            out_specs=[
                spot,
                pl.BlockSpec((step, columns), lambda r, order: (r, 0)),
                pl.BlockSpec((8, columns), lambda r, order: (0, 0)),
            ],
        ),
        out_shape=[
            jax.ShapeDtypeStruct(momentum.shape, jnp.float32),
            jax.ShapeDtypeStruct((rows, columns), jnp.bfloat16),
            jax.ShapeDtypeStruct((8, columns), jnp.float32),
        ],
        input_output_aliases=aliases,
        compiler_params=pltpu.CompilerParams(vmem_limit_bytes=VMEM_BYTES),
        cost_estimate=pl.CostEstimate(
            flops=4 * rows * columns, bytes_accessed=12 * rows * columns, transcendentals=0
        ),
        name="momentum",
    )(*operands)


def block_places(columns):
    count = columns // BLOCK
    return [(i, j) for i in range(count) for j in range(i, count)]


def gram_kernel(rows_ref, first_ref, second_ref):
    columns = rows_ref.shape[1]
    count = columns // BLOCK
    half = first_ref.shape[0]
    place = 0
    for i in range(count):
        turned = rows_ref[:, i * BLOCK : (i + 1) * BLOCK].T
        for j in range(i, count):
            block = jnp.dot(
                turned,
                rows_ref[:, j * BLOCK : (j + 1) * BLOCK],
                preferred_element_type=jnp.float32,
            ).astype(jnp.bfloat16)
            if place < half:
                first_ref[place] = block
            else:
                second_ref[place - half] = block
            place += 1


def gram_step(moved):
    rows, columns = moved.shape
    half = len(block_places(columns)) // 2
    part = jax.ShapeDtypeStruct((half, BLOCK, BLOCK), jnp.bfloat16)
    return pl.pallas_call(
        gram_kernel,
        in_specs=[pl.BlockSpec(memory_space=pltpu.VMEM)],
        out_specs=[pl.BlockSpec(memory_space=pltpu.VMEM)] * 2,
        out_shape=[part, part],
        compiler_params=pltpu.CompilerParams(vmem_limit_bytes=VMEM_BYTES),
        cost_estimate=pl.CostEstimate(
            flops=4 * half * BLOCK * BLOCK * rows,
            bytes_accessed=2 * rows * columns + 4 * half * BLOCK * BLOCK,
            transcendentals=0,
        ),
        name="gram",
    )(moved)


def times_gram(left_ref, gram_ref, j):
    start = j * BLOCK
    stop = start + BLOCK
    total = lax.dot_general(
        left_ref[:, start:],
        gram_ref[start:stop, start:],
        (((1,), (1,)), ((), ())),
        preferred_element_type=jnp.float32,
    )
    if j > 0:
        total += jnp.dot(
            left_ref[:, :start], gram_ref[:start, start:stop], preferred_element_type=jnp.float32
        )
    return total


def update_kernel(slot_ref, place_ref, factor_ref, rows_ref, *refs):
    pieces = refs[:4]
    out_ref, gram_ref, normal_ref, product_ref = refs[-4:]
    piece_blocks = pieces[0].shape[0]

    @pl.when(pl.program_id(0) == 0)
    def _():
        for number, piece in enumerate(pieces):
            for block in range(piece_blocks):
                index = number * piece_blocks + block
                row = pl.multiple_of(place_ref[0, index], BLOCK)
                column = pl.multiple_of(place_ref[1, index], BLOCK)
                gram_ref[pl.ds(row, BLOCK), pl.ds(column, BLOCK)] = piece[block]

    factor = factor_ref[0]
    factor_squared = factor * factor
    normal_ref[...] = (rows_ref[...].astype(jnp.float32) * factor).astype(jnp.bfloat16)
    count = gram_ref.shape[0] // BLOCK
    for j in range(count):
        product = times_gram(normal_ref, gram_ref, j) * factor_squared
        product_ref[:, j * BLOCK : (j + 1) * BLOCK] = product.astype(jnp.bfloat16)
    for j in range(count):
        here = slice(j * BLOCK, (j + 1) * BLOCK)
        second = times_gram(product_ref, gram_ref, j) * factor_squared
        orthogonal = (
            3.4445 * normal_ref[:, here].astype(jnp.float32)
            - 4.775 * product_ref[:, here].astype(jnp.float32)
            + 2.0315 * second
        )
        out_ref[0, :, here] = (orthogonal * math.sqrt(D)).astype(jnp.bfloat16)


def update_step(slot, places, factor, moved, pieces, earlier, local_count):
    rows, columns = moved.shape
    step = rows // 2 if rows % 32 == 0 and rows >= 512 else rows
    whole = pl.BlockSpec(pieces[0].shape, lambda r, *_: (0, 0, 0))
    in_specs = [
        pl.BlockSpec(memory_space=pltpu.SMEM),
        pl.BlockSpec((step, columns), lambda r, *_: (r, 0)),
    ] + [whole] * 4
    operands = [slot, places, factor, moved, *pieces]
    aliases = {}
    if earlier is not None:
        in_specs.append(pl.BlockSpec(memory_space=pl.ANY))
        operands.append(earlier)
        aliases = {8: 0}
    return pl.pallas_call(
        update_kernel,
        grid_spec=pltpu.PrefetchScalarGridSpec(
            num_scalar_prefetch=2,
            grid=(rows // step,),
            in_specs=in_specs,
            out_specs=pl.BlockSpec((1, step, columns), lambda r, slot, *_: (slot[0], r, 0)),
            scratch_shapes=[
                pltpu.VMEM((columns, columns), jnp.bfloat16),
                pltpu.VMEM((step, columns), jnp.bfloat16),
                pltpu.VMEM((step, columns), jnp.bfloat16),
            ],
        ),
        out_shape=jax.ShapeDtypeStruct((local_count, rows, columns), jnp.bfloat16),
        input_output_aliases=aliases,
        compiler_params=pltpu.CompilerParams(vmem_limit_bytes=VMEM_BYTES),
        cost_estimate=pl.CostEstimate(
            flops=4 * rows * columns * columns,
            bytes_accessed=4 * rows * columns + columns * columns,
            transcendentals=0,
        ),
        name="update",
    )(*operands)


def add_up(mine, arrived):
    return (mine.astype(jnp.float32) + arrived.astype(jnp.float32)).astype(jnp.bfloat16)


class Routes:
    def __init__(self, dp_count):
        everyone = range(dp_count)
        line = lambda i: i >> 1 & 3
        self.side = [(i, i ^ 1) for i in everyone]
        self.inner_side = [(i, i ^ 1) for i in everyone if line(i) in (1, 2)]
        self.inward = [(i, i + 2) for i in everyone if line(i) == 0]
        self.inward += [(i, i - 2) for i in everyone if line(i) == 3]
        self.outward = [(b, a) for a, b in self.inward]
        self.middle = [(i, i + 2) for i in everyone if line(i) == 1]
        self.middle += [(i, i - 2) for i in everyone if line(i) == 2]
        self.far = []
        distance = 8
        while distance < dp_count:
            self.far.append([(i, i ^ distance) for i in everyone])
            distance *= 2


def send(value, pairs):
    return lax.ppermute(value, "dp", pairs)


def halves(part, upper):
    count = part.shape[0] // 2
    kept = lax.dynamic_slice_in_dim(part, upper * count, count)
    given = lax.dynamic_slice_in_dim(part, (1 - upper) * count, count)
    return kept, given


def sum_side_first(part, routes, side, inner):
    kept, given = halves(part, side)
    total = add_up(kept, send(given, routes.side))
    total = add_up(total, send(total, routes.inward))
    total = add_up(total, send(total, routes.middle))
    for pairs in routes.far:
        total = add_up(total, send(total, pairs))
    total = jnp.where(inner, total, send(total, routes.outward))
    return total, send(total, routes.side)


def sum_line_first(part, routes, upper_line, inner):
    kept, given = halves(part, upper_line)
    given = add_up(given, send(given, routes.inward))
    kept = add_up(kept, send(kept, routes.inward))
    total = add_up(kept, send(given, routes.middle))
    total = add_up(total, send(total, routes.inner_side))
    for pairs in routes.far:
        total = add_up(total, send(total, pairs))
    other = send(total, routes.middle)
    total = jnp.where(inner, total, send(total, routes.outward))
    other = jnp.where(inner, other, send(other, routes.outward))
    return total, other


def shards(grad, momentum, placement):
    local_count, row_count, columns = grad.shape
    dp_count = lax.axis_size("dp")
    group_count = lax.axis_size("expert")
    routes = Routes(dp_count)
    my_group = lax.axis_index("expert")
    my_index = lax.axis_index("dp")
    side = my_index & 1
    line = my_index >> 1 & 3
    upper_line = line >> 1
    inner = (line == 1) | (line == 2)

    slot_ids = lax.iota(jnp.int32, local_count)
    moves = placement.reshape(group_count, local_count)

    def route(group, target):
        row = lax.dynamic_index_in_dim(moves, group, keepdims=False)
        chosen = row // local_count == target
        old_slot = jnp.sum(jnp.where(chosen, slot_ids, 0))
        new_slot = jnp.sum(jnp.where(chosen, row % local_count, 0))
        return old_slot, new_slot

    momentum_new = None
    outgoing = []
    squares = jnp.zeros((group_count, local_count), jnp.float32)
    for step in range(group_count):
        old_slot, _ = route(my_group, my_group ^ step)
        momentum_new, moved, sums = momentum_step(
            old_slot.reshape(1), grad, momentum, momentum_new
        )
        outgoing.append(moved)
        squares = squares.at[my_group, old_slot].add(jnp.sum(sums))
    squares = lax.psum(squares, ("dp", "expert"))
    factors = 0.5 * math.sqrt(columns) / jnp.sqrt(squares + 1e-06)

    owned = [outgoing[0]]
    for step in range(1, group_count):
        pairs = [(group, group ^ step) for group in range(group_count)]
        owned.append(lax.ppermute(outgoing[step], "expert", pairs))

    places = jnp.array(block_places(columns), jnp.int32) * BLOCK
    quarter = places.shape[0] // 4
    quarters = places.reshape(4, quarter, 2)
    order = jnp.stack([side, 1 - side, 2 + upper_line, 3 - upper_line])
    my_places = jnp.take(quarters, order, axis=0).reshape(4 * quarter, 2).T

    sums = []
    for step in range(group_count):
        first, second = gram_step(owned[step])
        pieces = sum_side_first(first, routes, side, inner)
        pieces += sum_line_first(second, routes, upper_line, inner)
        sums.append(pieces)

    update = None
    for step in range(group_count):
        group = my_group ^ step
        old_slot, new_slot = route(group, my_group)
        factor = lax.dynamic_slice(factors, (group, old_slot), (1, 1)).reshape(1)
        update = update_step(
            new_slot.reshape(1), my_places, factor, owned[step], sums[step], update, local_count
        )
    return momentum_new, update


def solution(mesh):
    return jax.shard_map(
        shards,
        mesh=mesh,
        in_specs=(P("expert", "dp", None), P("expert", "dp", None), P()),
        out_specs=(P("expert", "dp", None), P("expert", "dp", None)),
        check_vma=False,
    )
```

```python
import functools
import math

import jax
import jax.numpy as jnp
from jax import lax
from jax.experimental import pallas as pl
from jax.experimental.pallas import tpu as pltpu
from jax.sharding import PartitionSpec as P

D = 7168
BLOCK = 256
VMEM_BYTES = 56 * 2**20


def row_block(rows, most):
    for size in range(most, 15, -16):
        if rows % size == 0:
            return size
    return rows


def momentum_kernel(grad_ref, momentum_ref, new_ref, moved_ref, squares_ref):
    new = 0.95 * momentum_ref[0] + grad_ref[0].astype(jnp.float32)
    new_ref[0] = new
    moved = new.astype(jnp.bfloat16)
    moved_ref[0] = moved
    values = moved.astype(jnp.float32)
    rows, columns = values.shape
    partial_sum = jnp.sum((values * values).reshape(rows // 8, 8, columns), axis=0)

    @pl.when(pl.program_id(1) == 0)
    def _():
        squares_ref[0] = partial_sum

    @pl.when(pl.program_id(1) > 0)
    def _():
        squares_ref[0] += partial_sum


def momentum_step(grad, momentum):
    count, rows, columns = grad.shape
    step = row_block(rows, 128)
    spot = pl.BlockSpec((1, step, columns), lambda e, r: (e, r, 0))
    return pl.pallas_call(
        momentum_kernel,
        grid=(count, rows // step),
        in_specs=[spot, spot],
        out_specs=[spot, spot, pl.BlockSpec((1, 8, columns), lambda e, r: (e, 0, 0))],
        out_shape=[
            jax.ShapeDtypeStruct(momentum.shape, jnp.float32),
            jax.ShapeDtypeStruct(grad.shape, jnp.bfloat16),
            jax.ShapeDtypeStruct((count, 8, columns), jnp.float32),
        ],
        compiler_params=pltpu.CompilerParams(vmem_limit_bytes=VMEM_BYTES),
        cost_estimate=pl.CostEstimate(
            flops=4 * count * rows * columns,
            bytes_accessed=12 * count * rows * columns,
            transcendentals=0,
        ),
        name="momentum",
    )(grad, momentum)


def block_places(columns):
    count = columns // BLOCK
    return [(i, j) for i in range(count) for j in range(i, count)]


def gram_kernel(slot_ref, rows_ref, out_ref):
    columns = rows_ref.shape[2]
    count = columns // BLOCK
    place = 0
    for i in range(count):
        turned = rows_ref[0, :, i * BLOCK : (i + 1) * BLOCK].T
        for j in range(i, count):
            out_ref[place] = jnp.dot(
                turned,
                rows_ref[0, :, j * BLOCK : (j + 1) * BLOCK],
                preferred_element_type=jnp.float32,
            ).astype(jnp.bfloat16)
            place += 1


def gram_step(slot, moved):
    _, rows, columns = moved.shape
    blocks = len(block_places(columns))
    return pl.pallas_call(
        gram_kernel,
        grid_spec=pltpu.PrefetchScalarGridSpec(
            num_scalar_prefetch=1,
            grid=(1,),
            in_specs=[pl.BlockSpec((1, rows, columns), lambda _, slot: (slot[0], 0, 0))],
            out_specs=pl.BlockSpec((blocks, BLOCK, BLOCK), lambda _, slot: (0, 0, 0)),
        ),
        out_shape=jax.ShapeDtypeStruct((blocks, BLOCK, BLOCK), jnp.bfloat16),
        compiler_params=pltpu.CompilerParams(vmem_limit_bytes=VMEM_BYTES),
        cost_estimate=pl.CostEstimate(
            flops=2 * blocks * BLOCK * BLOCK * rows,
            bytes_accessed=2 * rows * columns + 2 * blocks * BLOCK * BLOCK,
            transcendentals=0,
        ),
        name="gram",
    )(slot, moved)


def times_gram(left_ref, gram_ref, j):
    start = j * BLOCK
    stop = start + BLOCK
    total = lax.dot_general(
        left_ref[:, start:],
        gram_ref[start:stop, start:],
        (((1,), (1,)), ((), ())),
        preferred_element_type=jnp.float32,
    )
    if j > 0:
        total += jnp.dot(
            left_ref[:, :start], gram_ref[:start, start:stop], preferred_element_type=jnp.float32
        )
    return total


def update_kernel(slots_ref, factor_ref, rows_ref, packed_ref, *refs):
    out_ref, gram_ref, normal_ref, product_ref = refs[-4:]

    @pl.when(pl.program_id(0) == 0)
    def _():
        for place, (i, j) in enumerate(block_places(gram_ref.shape[0])):
            gram_ref[i * BLOCK : (i + 1) * BLOCK, j * BLOCK : (j + 1) * BLOCK] = packed_ref[place]

    factor = factor_ref[0]
    factor_squared = factor * factor
    normal_ref[...] = (rows_ref[0].astype(jnp.float32) * factor).astype(jnp.bfloat16)
    count = gram_ref.shape[0] // BLOCK
    for j in range(count):
        product = times_gram(normal_ref, gram_ref, j) * factor_squared
        product_ref[:, j * BLOCK : (j + 1) * BLOCK] = product.astype(jnp.bfloat16)
    for j in range(count):
        here = slice(j * BLOCK, (j + 1) * BLOCK)
        second = times_gram(product_ref, gram_ref, j) * factor_squared
        orthogonal = (
            3.4445 * normal_ref[:, here].astype(jnp.float32)
            - 4.775 * product_ref[:, here].astype(jnp.float32)
            + 2.0315 * second
        )
        out_ref[0, :, here] = (orthogonal * math.sqrt(D)).astype(jnp.bfloat16)


def update_step(slots, factor, moved, packed, earlier=None):
    count, rows, columns = moved.shape
    step = rows // 2 if rows % 32 == 0 and rows >= 512 else rows
    in_specs = [
        pl.BlockSpec(memory_space=pltpu.SMEM),
        pl.BlockSpec((1, step, columns), lambda r, slots: (slots[0], r, 0)),
        pl.BlockSpec(packed.shape, lambda r, slots: (0, 0, 0)),
    ]
    operands = [slots, factor, moved, packed]
    aliases = {}
    if earlier is not None:
        in_specs.append(pl.BlockSpec(memory_space=pl.ANY))
        operands.append(earlier)
        aliases = {4: 0}
    else:
        count = 1
    return pl.pallas_call(
        update_kernel,
        grid_spec=pltpu.PrefetchScalarGridSpec(
            num_scalar_prefetch=1,
            grid=(rows // step,),
            in_specs=in_specs,
            out_specs=pl.BlockSpec((1, step, columns), lambda r, slots: (slots[1], r, 0)),
            scratch_shapes=[
                pltpu.VMEM((columns, columns), jnp.bfloat16),
                pltpu.VMEM((step, columns), jnp.bfloat16),
                pltpu.VMEM((step, columns), jnp.bfloat16),
            ],
        ),
        out_shape=jax.ShapeDtypeStruct((count, rows, columns), jnp.bfloat16),
        input_output_aliases=aliases,
        compiler_params=pltpu.CompilerParams(vmem_limit_bytes=VMEM_BYTES),
        cost_estimate=pl.CostEstimate(
            flops=4 * rows * columns * columns,
            bytes_accessed=4 * rows * columns + columns * columns,
            transcendentals=0,
        ),
        name="update",
    )(*operands)


def place_kernel(slot_ref, arrived_ref, *refs):
    refs[-1][...] = arrived_ref[...]


def place_step(slot, arrived, earlier, count):
    _, rows, columns = arrived.shape
    step = row_block(rows, 256)
    in_specs = [pl.BlockSpec((1, step, columns), lambda r, slot: (0, r, 0))]
    operands = [slot, arrived]
    aliases = {}
    if earlier is not None:
        in_specs.append(pl.BlockSpec(memory_space=pl.ANY))
        operands.append(earlier)
        aliases = {2: 0}
    return pl.pallas_call(
        place_kernel,
        grid_spec=pltpu.PrefetchScalarGridSpec(
            num_scalar_prefetch=1,
            grid=(rows // step,),
            in_specs=in_specs,
            out_specs=pl.BlockSpec((1, step, columns), lambda r, slot: (slot[0], r, 0)),
        ),
        out_shape=jax.ShapeDtypeStruct((count, rows, columns), jnp.bfloat16),
        input_output_aliases=aliases,
        compiler_params=pltpu.CompilerParams(vmem_limit_bytes=VMEM_BYTES),
        cost_estimate=pl.CostEstimate(
            flops=0, bytes_accessed=4 * rows * columns, transcendentals=0
        ),
        name="place",
    )(*operands)


def sum_over_dp(packed):
    flat = packed.reshape(-1, BLOCK)
    share = lax.psum_scatter(flat, "dp", scatter_dimension=0, tiled=True)
    return lax.all_gather(share, "dp", axis=0, tiled=True).reshape(packed.shape)


def shards(grad, momentum, placement):
    local_count, row_count, columns = grad.shape
    group_count = lax.axis_size("expert")
    my_group = lax.axis_index("expert")
    slot_ids = lax.iota(jnp.int32, local_count)
    moves = placement.reshape(group_count, local_count)

    def route(group, target):
        row = lax.dynamic_index_in_dim(moves, group, keepdims=False)
        chosen = row // local_count == target
        old_slot = jnp.sum(jnp.where(chosen, slot_ids, 0))
        new_slot = jnp.sum(jnp.where(chosen, row % local_count, 0))
        return old_slot, new_slot

    momentum_new, moved, sums = momentum_step(grad, momentum)
    squares = lax.psum(jnp.sum(sums, axis=(1, 2)), "dp")
    moved, squares = lax.optimization_barrier((moved, squares))
    factors = 0.5 * math.sqrt(columns) / jnp.sqrt(squares + 1e-06)

    steps = [step for step in range(group_count - 1, -1, -1)]
    old_slots = {step: route(my_group, my_group ^ step)[0] for step in steps}
    new_slots = {step: route(my_group ^ step, my_group)[1] for step in steps}
    grams = {step: gram_step(old_slots[step].reshape(1), moved) for step in steps}
    grams = {step: sum_over_dp(grams[step]) for step in steps}
    update = None
    for step in steps:
        old_slot = old_slots[step]
        factor = lax.dynamic_index_in_dim(factors, old_slot)
        if step == 0:
            slots = jnp.stack([old_slot, new_slots[0]])
            update = update_step(slots, factor, moved, grams[step], update)
        else:
            slots = jnp.stack([old_slot, 0])
            mine = update_step(slots, factor, moved, grams[step])
            pairs = [(group, group ^ step) for group in range(group_count)]
            arrived = lax.ppermute(mine, "expert", pairs)
            update = place_step(new_slots[step].reshape(1), arrived, update, local_count)
    return momentum_new, update


def solution(mesh):
    return jax.shard_map(
        shards,
        mesh=mesh,
        in_specs=(P("expert", "dp", None), P("expert", "dp", None), P()),
        out_specs=(P("expert", "dp", None), P("expert", "dp", None)),
        check_vma=False,
    )
```

```python
import functools
import math

import jax
import jax.numpy as jnp
from jax import lax
from jax.experimental import pallas as pl
from jax.experimental.pallas import tpu as pltpu
from jax.sharding import PartitionSpec as P

D = 7168
BLOCK = 256
TRAVEL = 3
VMEM_BYTES = 56 * 2**20


def row_block(rows, most):
    for size in range(most, 15, -16):
        if rows % size == 0:
            return size
    return rows


def momentum_kernel(order_ref, grad_ref, momentum_ref, *refs):
    new_ref, moved_ref, squares_ref = refs[-3:]
    new = 0.95 * momentum_ref[0] + grad_ref[0].astype(jnp.float32)
    new_ref[0] = new
    moved = new.astype(jnp.bfloat16)
    moved_ref[...] = moved
    values = moved.astype(jnp.float32)
    rows, columns = values.shape
    partial_sum = jnp.sum((values * values).reshape(rows // 8, 8, columns), axis=0)

    @pl.when(pl.program_id(0) == 0)
    def _():
        squares_ref[...] = partial_sum

    @pl.when(pl.program_id(0) > 0)
    def _():
        squares_ref[...] += partial_sum


def momentum_step(source, grad, momentum, earlier):
    local_count, rows, columns = grad.shape
    step = row_block(rows, 128)
    spot = pl.BlockSpec((1, step, columns), lambda r, order: (order[0], r, 0))
    in_specs = [spot, spot]
    operands = [source, grad, momentum]
    aliases = {}
    if earlier is not None:
        in_specs.append(pl.BlockSpec(memory_space=pl.ANY))
        operands.append(earlier)
        aliases = {3: 0}
    return pl.pallas_call(
        momentum_kernel,
        grid_spec=pltpu.PrefetchScalarGridSpec(
            num_scalar_prefetch=1,
            grid=(rows // step,),
            in_specs=in_specs,
            out_specs=[
                spot,
                pl.BlockSpec((step, columns), lambda r, order: (r, 0)),
                pl.BlockSpec((8, columns), lambda r, order: (0, 0)),
            ],
        ),
        out_shape=[
            jax.ShapeDtypeStruct(momentum.shape, jnp.float32),
            jax.ShapeDtypeStruct((rows, columns), jnp.bfloat16),
            jax.ShapeDtypeStruct((8, columns), jnp.float32),
        ],
        input_output_aliases=aliases,
        compiler_params=pltpu.CompilerParams(vmem_limit_bytes=VMEM_BYTES),
        cost_estimate=pl.CostEstimate(
            flops=4 * rows * columns, bytes_accessed=12 * rows * columns, transcendentals=0
        ),
        name="momentum",
    )(*operands)


def block_places(columns):
    count = columns // BLOCK
    return [(i, j) for i in range(count) for j in range(i, count)]


def gram_kernel(rows_ref, first_ref, second_ref):
    columns = rows_ref.shape[1]
    count = columns // BLOCK
    half = first_ref.shape[0]
    place = 0
    for i in range(count):
        turned = rows_ref[:, i * BLOCK : (i + 1) * BLOCK].T
        for j in range(i, count):
            block = jnp.dot(
                turned,
                rows_ref[:, j * BLOCK : (j + 1) * BLOCK],
                preferred_element_type=jnp.float32,
            ).astype(jnp.bfloat16)
            if place < half:
                first_ref[place] = block
            else:
                second_ref[place - half] = block
            place += 1


def gram_step(moved):
    rows, columns = moved.shape
    half = len(block_places(columns)) // 2
    part = jax.ShapeDtypeStruct((half, BLOCK, BLOCK), jnp.bfloat16)
    return pl.pallas_call(
        gram_kernel,
        in_specs=[pl.BlockSpec(memory_space=pltpu.VMEM)],
        out_specs=[pl.BlockSpec(memory_space=pltpu.VMEM)] * 2,
        out_shape=[part, part],
        compiler_params=pltpu.CompilerParams(vmem_limit_bytes=VMEM_BYTES),
        cost_estimate=pl.CostEstimate(
            flops=4 * half * BLOCK * BLOCK * rows,
            bytes_accessed=2 * rows * columns + 4 * half * BLOCK * BLOCK,
            transcendentals=0,
        ),
        name="gram",
    )(moved)


def times_gram(left_ref, gram_ref, j):
    start = j * BLOCK
    stop = start + BLOCK
    total = lax.dot_general(
        left_ref[:, start:],
        gram_ref[start:stop, start:],
        (((1,), (1,)), ((), ())),
        preferred_element_type=jnp.float32,
    )
    if j > 0:
        total += jnp.dot(
            left_ref[:, :start], gram_ref[:start, start:stop], preferred_element_type=jnp.float32
        )
    return total


def update_kernel(slot_ref, place_ref, factor_ref, rows_ref, *refs):
    pieces = refs[:4]
    out_ref, gram_ref, normal_ref, product_ref = refs[-4:]
    piece_blocks = pieces[0].shape[0]

    @pl.when(pl.program_id(0) == 0)
    def _():
        for number, piece in enumerate(pieces):
            for block in range(piece_blocks):
                index = number * piece_blocks + block
                row = pl.multiple_of(place_ref[0, index], BLOCK)
                column = pl.multiple_of(place_ref[1, index], BLOCK)
                gram_ref[pl.ds(row, BLOCK), pl.ds(column, BLOCK)] = piece[block]

    factor = factor_ref[0]
    factor_squared = factor * factor
    normal_ref[...] = (rows_ref[...].astype(jnp.float32) * factor).astype(jnp.bfloat16)
    count = gram_ref.shape[0] // BLOCK
    for j in range(count):
        product = times_gram(normal_ref, gram_ref, j) * factor_squared
        product_ref[:, j * BLOCK : (j + 1) * BLOCK] = product.astype(jnp.bfloat16)
    for j in range(count):
        here = slice(j * BLOCK, (j + 1) * BLOCK)
        second = times_gram(product_ref, gram_ref, j) * factor_squared
        orthogonal = (
            3.4445 * normal_ref[:, here].astype(jnp.float32)
            - 4.775 * product_ref[:, here].astype(jnp.float32)
            + 2.0315 * second
        )
        out_ref[0, :, here] = (orthogonal * math.sqrt(D)).astype(jnp.bfloat16)


def update_step(slot, places, factor, moved, pieces, earlier=None, count=1):
    rows, columns = moved.shape
    step = rows // 2 if rows % 32 == 0 and rows >= 512 else rows
    whole = pl.BlockSpec(pieces[0].shape, lambda r, *_: (0, 0, 0))
    in_specs = [
        pl.BlockSpec(memory_space=pltpu.SMEM),
        pl.BlockSpec((step, columns), lambda r, *_: (r, 0)),
    ] + [whole] * 4
    operands = [slot, places, factor, moved, *pieces]
    aliases = {}
    if earlier is not None:
        in_specs.append(pl.BlockSpec(memory_space=pl.ANY))
        operands.append(earlier)
        aliases = {8: 0}
    return pl.pallas_call(
        update_kernel,
        grid_spec=pltpu.PrefetchScalarGridSpec(
            num_scalar_prefetch=2,
            grid=(rows // step,),
            in_specs=in_specs,
            out_specs=pl.BlockSpec((1, step, columns), lambda r, slot, *_: (slot[0], r, 0)),
            scratch_shapes=[
                pltpu.VMEM((columns, columns), jnp.bfloat16),
                pltpu.VMEM((step, columns), jnp.bfloat16),
                pltpu.VMEM((step, columns), jnp.bfloat16),
            ],
        ),
        out_shape=jax.ShapeDtypeStruct((count, rows, columns), jnp.bfloat16),
        input_output_aliases=aliases,
        compiler_params=pltpu.CompilerParams(vmem_limit_bytes=VMEM_BYTES),
        cost_estimate=pl.CostEstimate(
            flops=rows * columns * columns // 4, bytes_accessed=rows * columns, transcendentals=0
        ),
        name="update",
    )(*operands)


def place_kernel(slot_ref, arrived_ref, *refs):
    refs[-1][...] = arrived_ref[...]


def place_step(slot, arrived, earlier, count):
    _, rows, columns = arrived.shape
    step = row_block(rows, 256)
    in_specs = [pl.BlockSpec((1, step, columns), lambda r, slot: (0, r, 0))]
    operands = [slot, arrived]
    aliases = {}
    if earlier is not None:
        in_specs.append(pl.BlockSpec(memory_space=pl.ANY))
        operands.append(earlier)
        aliases = {2: 0}
    return pl.pallas_call(
        place_kernel,
        grid_spec=pltpu.PrefetchScalarGridSpec(
            num_scalar_prefetch=1,
            grid=(rows // step,),
            in_specs=in_specs,
            out_specs=pl.BlockSpec((1, step, columns), lambda r, slot: (slot[0], r, 0)),
        ),
        out_shape=jax.ShapeDtypeStruct((count, rows, columns), jnp.bfloat16),
        input_output_aliases=aliases,
        compiler_params=pltpu.CompilerParams(vmem_limit_bytes=VMEM_BYTES),
        cost_estimate=pl.CostEstimate(
            flops=0, bytes_accessed=4 * rows * columns, transcendentals=0
        ),
        name="place",
    )(*operands)


def add_up(mine, arrived):
    return (mine.astype(jnp.float32) + arrived.astype(jnp.float32)).astype(jnp.bfloat16)


class Routes:
    def __init__(self, dp_count):
        everyone = range(dp_count)
        line = lambda i: i >> 1 & 3
        self.side = [(i, i ^ 1) for i in everyone]
        self.inner_side = [(i, i ^ 1) for i in everyone if line(i) in (1, 2)]
        self.inward = [(i, i + 2) for i in everyone if line(i) == 0]
        self.inward += [(i, i - 2) for i in everyone if line(i) == 3]
        self.outward = [(b, a) for a, b in self.inward]
        self.middle = [(i, i + 2) for i in everyone if line(i) == 1]
        self.middle += [(i, i - 2) for i in everyone if line(i) == 2]
        self.swaps = [[(i, i ^ 1 << bit) for i in everyone] for bit in range(dp_count.bit_length() - 1)]
        self.far = []
        distance = 8
        while distance < dp_count:
            self.far.append([(i, i ^ distance) for i in everyone])
            distance *= 2


def send(value, pairs):
    return lax.ppermute(value, "dp", pairs)


def halves(part, upper):
    count = part.shape[0] // 2
    kept = lax.dynamic_slice_in_dim(part, upper * count, count)
    given = lax.dynamic_slice_in_dim(part, (1 - upper) * count, count)
    return kept, given


class SideFirst:
    hops = {
        "side": ("side", ()),
        "in": ("inward", ("side",)),
        "middle": ("middle", ("in",)),
        "out": ("outward", ("middle",)),
        "gather": ("side", ("out",)),
    }

    def __init__(self, routes, place, part):
        self.routes = routes
        self.inner = place.inner
        self.kept, self.given = halves(part, place.side)

    def value(self, hop, got):
        if hop == "side":
            return self.given
        if hop == "in":
            self.total = add_up(self.kept, got["side"])
        elif hop == "middle":
            self.total = add_up(self.total, got["in"])
        elif hop == "out":
            self.total = add_up(self.total, got["middle"])
            for pairs in self.routes.far:
                self.total = add_up(self.total, send(self.total, pairs))
        else:
            self.total = jnp.where(self.inner, self.total, got["out"])
        return self.total

    def pieces(self, got):
        return self.total, got["gather"]


class LineFirst:
    hops = {
        "in given": ("inward", ()),
        "in kept": ("inward", ()),
        "middle": ("middle", ("in given",)),
        "side": ("inner_side", ("in kept", "middle")),
        "middle back": ("middle", ("side",)),
        "out": ("outward", ("side",)),
        "out other": ("outward", ("middle back",)),
    }

    def __init__(self, routes, place, part):
        self.routes = routes
        self.inner = place.inner
        self.kept, self.given = halves(part, place.upper_line)
        self.total = None

    def value(self, hop, got):
        if hop == "in given":
            return self.given
        if hop == "in kept":
            return self.kept
        if hop == "middle":
            return add_up(self.given, got["in given"])
        if hop == "side":
            self.kept = add_up(add_up(self.kept, got["in kept"]), got["middle"])
            return self.kept
        if hop == "out other":
            return got["middle back"]
        if self.total is None:
            self.total = add_up(self.kept, got["side"])
            for pairs in self.routes.far:
                self.total = add_up(self.total, send(self.total, pairs))
        return self.total

    def pieces(self, got):
        return (
            jnp.where(self.inner, self.total, got["out"]),
            jnp.where(self.inner, got["middle back"], got["out other"]),
        )


def plan(experts):
    hops = {}
    for expert in range(experts):
        for kind in (LineFirst, SideFirst):
            for name, (link, needs) in kind.hops.items():
                needed = [(expert, kind, need) for need in needs]
                hops[expert, kind, name] = (link.replace("inner_", ""), needed)

    def length(hop):
        return 1 + max([length(h) for h in hops if hop in hops[h][1]], default=0)

    waiting = sorted(hops, key=lambda hop: (hop[0], -length(hop)))
    slot_of = {}
    slots = []
    while waiting:
        now = len(slots)
        taken = {}
        for hop in waiting:
            link, needed = hops[hop]
            in_time = hop[0] * 2 <= now and all(slot_of.get(h, now) < now for h in needed)
            if link not in taken and in_time:
                taken[link] = hop
        for hop in taken.values():
            slot_of[hop] = now
            waiting.remove(hop)
        slots.append(list(taken.values()))
    return slots


class Place:
    def __init__(self, index):
        line = index >> 1 & 3
        self.side = index & 1
        self.upper_line = line >> 1
        self.inner = (line == 1) | (line == 2)


def shards(grad, momentum, placement):
    local_count, row_count, columns = grad.shape
    group_count = lax.axis_size("expert")
    routes = Routes(lax.axis_size("dp"))
    my_group = lax.axis_index("expert")
    my_place = Place(lax.axis_index("dp"))

    slot_ids = lax.iota(jnp.int32, local_count)
    moves = placement.reshape(group_count, local_count)

    def route(group, target):
        row = lax.dynamic_index_in_dim(moves, group, keepdims=False)
        chosen = row // local_count == target
        old_slot = jnp.sum(jnp.where(chosen, slot_ids, 0))
        new_slot = jnp.sum(jnp.where(chosen, row % local_count, 0))
        return old_slot, new_slot

    places = jnp.array(block_places(columns), jnp.int32) * BLOCK
    quarter = places.shape[0] // 4
    quarters = places.reshape(4, quarter, 2)
    order = jnp.stack(
        [my_place.side, 1 - my_place.side, 2 + my_place.upper_line, 3 - my_place.upper_line]
    )
    my_places = jnp.take(quarters, order, axis=0).reshape(4 * quarter, 2).T

    distances = list(range(group_count - 1, -1, -1))
    slots = plan(group_count)
    first_slot = [
        min(s for s, hops in enumerate(slots) if any(h[0] == e for h in hops))
        for e in range(group_count)
    ]
    last_slot = [
        max(s for s, hops in enumerate(slots) if any(h[0] == e for h in hops))
        for e in range(group_count)
    ]
    momentum_new = None
    update = None
    factors = None
    moved, partial_squares, chains, got, leaving = {}, {}, {}, {}, {}
    arrivals = []
    due = {now: [] for now in range(len(slots) + 8)}

    def after_arrivals(*values):
        return lax.optimization_barrier((values, arrivals))[0]

    def take_momentum(e, limit):
        nonlocal momentum_new
        old_slot, _ = route(my_group, my_group ^ distances[e])
        (old_slot,) = after_arrivals(old_slot.reshape(1))
        momentum_new, moved[e], sums = momentum_step(old_slot, grad, momentum, momentum_new)
        partial_squares[e] = jnp.sum(sums)
        due[limit].append(sums)

    def take_gram(e, limit):
        (rows,) = after_arrivals(moved[e])
        first, second = gram_step(rows)
        chains[e, SideFirst] = SideFirst(routes, my_place, first)
        chains[e, LineFirst] = LineFirst(routes, my_place, second)
        got[e, SideFirst], got[e, LineFirst] = {}, {}
        due[limit].append(second)

    def take_update(e, limit):
        nonlocal update
        pieces = chains[e, SideFirst].pieces(got[e, SideFirst])
        pieces += chains[e, LineFirst].pieces(got[e, LineFirst])
        pieces = after_arrivals(*pieces)
        new_slot = route(my_group ^ distances[e], my_group)[1].reshape(1)
        factor = factors[e].reshape(1)
        if distances[e] == 0:
            update = update_step(
                new_slot, my_places, factor, moved[e], pieces, update, local_count
            )
            return
        here = jnp.zeros((1,), jnp.int32)
        mine = update_step(here, my_places, factor, moved[e], pieces)
        due[limit].append(mine)
        pairs = [(g, g ^ distances[e]) for g in range(group_count)]
        arrived = lax.ppermute(mine, "expert", pairs)
        leaving[e] = new_slot, arrived
        due[limit + TRAVEL].append(arrived)

    def take_place(e, limit):
        nonlocal update
        new_slot, arrived = leaving.pop(e)
        (new_slot,) = after_arrivals(new_slot)
        update = place_step(new_slot, arrived, update, local_count)
        due[limit].append(update)

    take_momentum(0, 0)
    take_gram(0, 0)
    swaps = None
    for now, hops in enumerate(slots):
        values = [chains[e, kind].value(name, got[e, kind]) for e, kind, name in hops]
        values = lax.optimization_barrier((values, arrivals, due[now]))[0]
        if now + 1 < group_count:
            take_momentum(now + 1, now + 1)
        for e in range(1, group_count):
            if first_slot[e] == now + 2 or (now == 0 and first_slot[e] < 2):
                take_gram(e, now + 1)
        for e in list(leaving):
            if last_slot[e] + 2 + TRAVEL == now:
                take_place(e, now + 1)
        for e in range(group_count - 1):
            if last_slot[e] + 1 == now:
                take_update(e, now + 1)
        arrivals = []
        for (e, kind, name), value in zip(hops, values):
            arrival = send(value, getattr(routes, kind.hops[name][0]))
            got[e, kind][name] = arrival
            arrivals.append(arrival)
        if now + 1 == group_count:
            small = jnp.stack([partial_squares[e] for e in range(group_count)])
            swaps = list(routes.swaps)
            at_once = -(-len(swaps) // 3)
        if swaps:
            for _ in range(min(at_once, len(swaps))):
                arrival = send(small, swaps.pop())
                small = small + arrival
                arrivals.append(arrival)
            if not swaps:
                factors = 0.5 * math.sqrt(columns) / jnp.sqrt(small + 1e-06)
    for e in sorted(leaving):
        take_place(e, len(slots))
    take_update(group_count - 1, len(slots))
    return momentum_new, update


def solution(mesh):
    return jax.shard_map(
        shards,
        mesh=mesh,
        in_specs=(P("expert", "dp", None), P("expert", "dp", None), P()),
        out_specs=(P("expert", "dp", None), P("expert", "dp", None)),
        check_vma=False,
    )
```

```python
import functools
import math

import jax
import jax.numpy as jnp
from jax import lax
from jax.experimental import pallas as pl
from jax.experimental.pallas import tpu as pltpu
from jax.sharding import PartitionSpec as P

D = 7168
BLOCK = 256
VMEM_BYTES = 56 * 2**20
SMALL_COST = pl.CostEstimate(flops=2**20, bytes_accessed=2**10, transcendentals=0)


def row_block(rows, most):
    for size in range(most, 15, -16):
        if rows % size == 0:
            return size
    return rows


def momentum_kernel(order_ref, grad_ref, momentum_ref, *refs):
    new_ref, moved_ref, squares_ref = refs[-3:]
    new = 0.95 * momentum_ref[0] + grad_ref[0].astype(jnp.float32)
    new_ref[0] = new
    moved = new.astype(jnp.bfloat16)
    moved_ref[...] = moved
    values = moved.astype(jnp.float32)
    rows, columns = values.shape
    partial_sum = jnp.sum((values * values).reshape(rows // 8, 8, columns), axis=0)

    @pl.when(pl.program_id(0) == 0)
    def _():
        squares_ref[...] = partial_sum

    @pl.when(pl.program_id(0) > 0)
    def _():
        squares_ref[...] += partial_sum


def momentum_step(source, grad, momentum, earlier):
    local_count, rows, columns = grad.shape
    step = row_block(rows, 128)
    spot = pl.BlockSpec((1, step, columns), lambda r, order: (order[0], r, 0))
    in_specs = [spot, spot]
    operands = [source, grad, momentum]
    aliases = {}
    if earlier is not None:
        in_specs.append(pl.BlockSpec(memory_space=pl.ANY))
        operands.append(earlier)
        aliases = {3: 0}
    return pl.pallas_call(
        momentum_kernel,
        grid_spec=pltpu.PrefetchScalarGridSpec(
            num_scalar_prefetch=1,
            grid=(rows // step,),
            in_specs=in_specs,
            out_specs=[
                spot,
                pl.BlockSpec((step, columns), lambda r, order: (r, 0)),
                pl.BlockSpec((8, columns), lambda r, order: (0, 0)),
            ],
        ),
        out_shape=[
            jax.ShapeDtypeStruct(momentum.shape, jnp.float32),
            jax.ShapeDtypeStruct((rows, columns), jnp.bfloat16),
            jax.ShapeDtypeStruct((8, columns), jnp.float32),
        ],
        input_output_aliases=aliases,
        compiler_params=pltpu.CompilerParams(vmem_limit_bytes=VMEM_BYTES),
        cost_estimate=SMALL_COST,
        name="momentum",
    )(*operands)


def block_places(columns):
    count = columns // BLOCK
    return [(i, j) for i in range(count) for j in range(i, count)]


def gram_kernel(upper_ref, rows_ref, *refs):
    outputs, halves, sems = refs[:4], refs[4:6], refs[6]
    columns = rows_ref.shape[1]
    count = columns // BLOCK
    quarter = halves[0].shape[1]
    copies = []
    place = 0
    for i in range(count):
        turned = rows_ref[:, i * BLOCK : (i + 1) * BLOCK].T
        for j in range(i, count):
            half, inside = divmod(place, 2 * quarter)
            part, slot = divmod(inside, quarter)
            halves[half][part, slot] = jnp.dot(
                turned,
                rows_ref[:, j * BLOCK : (j + 1) * BLOCK],
                preferred_element_type=jnp.float32,
            ).astype(jnp.bfloat16)
            place += 1
            if place % (2 * quarter) == 0:
                upper = upper_ref[half]
                for given in range(2):
                    number = 2 * half + given
                    source = upper if given == 0 else 1 - upper
                    copy = pltpu.make_async_copy(
                        halves[half].at[source], outputs[number], sems.at[number]
                    )
                    copy.start()
                    copies.append(copy)
    for copy in copies:
        copy.wait()


def gram_step(uppers, moved):
    rows, columns = moved.shape
    quarter = len(block_places(columns)) // 4
    part = jax.ShapeDtypeStruct((quarter, BLOCK, BLOCK), jnp.bfloat16)
    return pl.pallas_call(
        gram_kernel,
        in_specs=[
            pl.BlockSpec(memory_space=pltpu.SMEM),
            pl.BlockSpec(memory_space=pltpu.VMEM),
        ],
        out_specs=[pl.BlockSpec(memory_space=pl.ANY)] * 4,
        out_shape=[part] * 4,
        scratch_shapes=[
            pltpu.VMEM((2, quarter, BLOCK, BLOCK), jnp.bfloat16),
            pltpu.VMEM((2, quarter, BLOCK, BLOCK), jnp.bfloat16),
            pltpu.SemaphoreType.DMA((4,)),
        ],
        compiler_params=pltpu.CompilerParams(vmem_limit_bytes=VMEM_BYTES),
        cost_estimate=SMALL_COST,
        name="gram",
    )(uppers, moved)


def times_gram(left_ref, gram_ref, j):
    start = j * BLOCK
    stop = start + BLOCK
    total = lax.dot_general(
        left_ref[:, start:],
        gram_ref[start:stop, start:],
        (((1,), (1,)), ((), ())),
        preferred_element_type=jnp.float32,
    )
    if j > 0:
        total += jnp.dot(
            left_ref[:, :start], gram_ref[:start, start:stop], preferred_element_type=jnp.float32
        )
    return total


def update_kernel(slot_ref, place_ref, factor_ref, rows_ref, *refs):
    pieces = refs[:4]
    out_ref, gram_ref, normal_ref, product_ref = refs[-4:]
    piece_blocks = pieces[0].shape[0]

    @pl.when(pl.program_id(0) == 0)
    def _():
        for number, piece in enumerate(pieces):
            for block in range(piece_blocks):
                index = number * piece_blocks + block
                row = pl.multiple_of(place_ref[0, index], BLOCK)
                column = pl.multiple_of(place_ref[1, index], BLOCK)
                gram_ref[pl.ds(row, BLOCK), pl.ds(column, BLOCK)] = piece[block]

    factor = factor_ref[0]
    factor_squared = factor * factor
    normal_ref[...] = (rows_ref[...].astype(jnp.float32) * factor).astype(jnp.bfloat16)
    count = gram_ref.shape[0] // BLOCK
    for j in range(count):
        product = times_gram(normal_ref, gram_ref, j) * factor_squared
        product_ref[:, j * BLOCK : (j + 1) * BLOCK] = product.astype(jnp.bfloat16)
    for j in range(count):
        here = slice(j * BLOCK, (j + 1) * BLOCK)
        second = times_gram(product_ref, gram_ref, j) * factor_squared
        orthogonal = (
            3.4445 * normal_ref[:, here].astype(jnp.float32)
            - 4.775 * product_ref[:, here].astype(jnp.float32)
            + 2.0315 * second
        )
        out_ref[0, :, here] = (orthogonal * math.sqrt(D)).astype(jnp.bfloat16)


def update_step(slot, places, factor, moved, pieces, earlier=None, count=1):
    rows, columns = moved.shape
    step = rows // 2 if rows % 32 == 0 and rows >= 512 else rows
    whole = pl.BlockSpec(pieces[0].shape, lambda r, *_: (0, 0, 0))
    in_specs = [
        pl.BlockSpec(memory_space=pltpu.SMEM),
        pl.BlockSpec((step, columns), lambda r, *_: (r, 0)),
    ] + [whole] * 4
    operands = [slot, places, factor, moved, *pieces]
    aliases = {}
    if earlier is not None:
        in_specs.append(pl.BlockSpec(memory_space=pl.ANY))
        operands.append(earlier)
        aliases = {8: 0}
    return pl.pallas_call(
        update_kernel,
        grid_spec=pltpu.PrefetchScalarGridSpec(
            num_scalar_prefetch=2,
            grid=(rows // step,),
            in_specs=in_specs,
            out_specs=pl.BlockSpec((1, step, columns), lambda r, slot, *_: (slot[0], r, 0)),
            scratch_shapes=[
                pltpu.VMEM((columns, columns), jnp.bfloat16),
                pltpu.VMEM((step, columns), jnp.bfloat16),
                pltpu.VMEM((step, columns), jnp.bfloat16),
            ],
        ),
        out_shape=jax.ShapeDtypeStruct((count, rows, columns), jnp.bfloat16),
        input_output_aliases=aliases,
        compiler_params=pltpu.CompilerParams(vmem_limit_bytes=VMEM_BYTES),
        cost_estimate=SMALL_COST,
        name="update",
    )(*operands)


def place_kernel(slot_ref, arrived_ref, *refs):
    refs[-1][...] = arrived_ref[...]


def place_step(slot, arrived, earlier, count):
    _, rows, columns = arrived.shape
    step = row_block(rows, 256)
    in_specs = [pl.BlockSpec((1, step, columns), lambda r, slot: (0, r, 0))]
    operands = [slot, arrived]
    aliases = {}
    if earlier is not None:
        in_specs.append(pl.BlockSpec(memory_space=pl.ANY))
        operands.append(earlier)
        aliases = {2: 0}
    return pl.pallas_call(
        place_kernel,
        grid_spec=pltpu.PrefetchScalarGridSpec(
            num_scalar_prefetch=1,
            grid=(rows // step,),
            in_specs=in_specs,
            out_specs=pl.BlockSpec((1, step, columns), lambda r, slot: (slot[0], r, 0)),
        ),
        out_shape=jax.ShapeDtypeStruct((count, rows, columns), jnp.bfloat16),
        input_output_aliases=aliases,
        compiler_params=pltpu.CompilerParams(vmem_limit_bytes=VMEM_BYTES),
        cost_estimate=SMALL_COST,
        name="place",
    )(*operands)


def add_up(mine, arrived):
    return (mine.astype(jnp.float32) + arrived.astype(jnp.float32)).astype(jnp.bfloat16)


class Routes:
    def __init__(self, dp_count):
        everyone = range(dp_count)
        line = lambda i: i >> 1 & 3
        self.side = [(i, i ^ 1) for i in everyone]
        self.inner_side = [(i, i ^ 1) for i in everyone if line(i) in (1, 2)]
        self.inward = [(i, i + 2) for i in everyone if line(i) == 0]
        self.inward += [(i, i - 2) for i in everyone if line(i) == 3]
        self.outward = [(b, a) for a, b in self.inward]
        self.middle = [(i, i + 2) for i in everyone if line(i) == 1]
        self.middle += [(i, i - 2) for i in everyone if line(i) == 2]
        self.swaps = [[(i, i ^ 1 << bit) for i in everyone] for bit in range(dp_count.bit_length() - 1)]
        self.far = []
        distance = 8
        while distance < dp_count:
            self.far.append([(i, i ^ distance) for i in everyone])
            distance *= 2


def send(value, pairs):
    return lax.ppermute(value, "dp", pairs)


class SideFirst:
    hops = {
        "side": ("side", (), 0),
        "in": ("inward", ("side",), 1),
        "middle": ("middle", ("in",), 1),
        "out": ("outward", ("middle",), 1),
        "gather": ("side", ("out",), 1),
    }

    def __init__(self, routes, place, kept, given):
        self.routes, self.inner = routes, place.inner
        self.kept, self.given = kept, given

    def value(self, hop, got):
        if hop == "side":
            return self.given
        if hop == "in":
            self.total = add_up(self.kept, got["side"])
        elif hop == "middle":
            self.total = add_up(self.total, got["in"])
        elif hop == "out":
            self.total = add_up(self.total, got["middle"])
            for pairs in self.routes.far:
                self.total = add_up(self.total, send(self.total, pairs))
        else:
            self.total = jnp.where(self.inner, self.total, got["out"])
        return self.total

    def pieces(self, got):
        return self.total, got["gather"]


class LineFirst:
    hops = {
        "in given": ("inward", (), 0),
        "in kept": ("inward", (), 0),
        "middle": ("middle", ("in given",), 1),
        "side": ("inner_side", ("in kept", "middle"), 2),
        "middle back": ("middle", ("side",), 1),
        "out": ("outward", ("side",), 0),
        "out other": ("outward", ("middle back",), 0),
    }

    def __init__(self, routes, place, kept, given):
        self.routes, self.inner = routes, place.inner
        self.kept, self.given = kept, given
        self.total = None

    def value(self, hop, got):
        if hop == "in given":
            return self.given
        if hop == "in kept":
            return self.kept
        if hop == "middle":
            return add_up(self.given, got["in given"])
        if hop == "side":
            self.kept = add_up(add_up(self.kept, got["in kept"]), got["middle"])
            return self.kept
        if hop == "out other":
            return got["middle back"]
        if self.total is None:
            self.total = add_up(self.kept, got["side"])
            for pairs in self.routes.far:
                self.total = add_up(self.total, send(self.total, pairs))
        return self.total

    def pieces(self, got):
        return (
            jnp.where(self.inner, self.total, got["out"]),
            jnp.where(self.inner, got["middle back"], got["out other"]),
        )


def plan(experts):
    transfer, latency, issue, pass_over = 23.3, 3.0, 1.5, 1.6
    takes = {"momentum": 12.0, "gram": 9.0, "update": 23.0, "place": 5.0}
    swaps_take, near, far = 30.0, 20.0, 78.0
    hops = {}
    for expert in range(experts):
        for kind in (LineFirst, SideFirst):
            for name, (link, needs, passes) in kind.hops.items():
                needed = [(expert, kind, need) for need in needs]
                hops[expert, kind, name] = (link.replace("inner_", ""), needed, passes)
    last_hops = {}

    def length(hop):
        if hop not in last_hops:
            later = [length(h) for h in hops if hop in hops[h][1]]
            last_hops[hop] = 1 + max(later, default=0)
        return last_hops[hop]

    first_choice = sorted(hops, key=lambda hop: (hop[0], -length(hop)))
    order = []
    now = 0.0
    count = dict.fromkeys(takes, 0)
    arrival = {}
    queues = {}
    update_arrival = {}
    far_free = 0.0

    def do(kernel):
        nonlocal now
        order.append((kernel, count[kernel]))
        count[kernel] += 1
        now += takes[kernel]

    def next_hop():
        for hop in first_choice:
            link, needed, _ = hops[hop]
            queued = sum(time > now for time in queues.setdefault(link, []))
            if hop[0] < count["gram"] and hop not in arrival and queued < 2:
                if all(arrival.get(need, math.inf) <= now for need in needed):
                    return hop
        return None

    do("momentum")
    do("gram")
    while count["update"] < experts:
        hop = next_hop()
        updating = count["update"]
        last = updating == experts - 1
        mine = [h for h in hops if h[0] == updating]
        whole = all(arrival.get(h, math.inf) <= now for h in mine)
        if hop is not None:
            link, _, passes = hops[hop]
            order.append(("hop", hop))
            now += issue + passes * pass_over
            queue = queues[link]
            queue.append(max([now + 1, *queue[-1:]]) + transfer)
            arrival[hop] = queue[-1] + latency
        elif count["gram"] < count["momentum"]:
            do("gram")
        elif count["momentum"] < experts:
            do("momentum")
            if count["momentum"] == experts:
                order.append(("swaps", 0))
                squares_arrival = now + swaps_take
        elif whole and squares_arrival <= now and (not last or count["place"] == updating):
            do("update")
            if updating < experts - 2:
                far_free = max(now, far_free) + far
                update_arrival[updating] = far_free
            else:
                update_arrival[updating] = now + near
        elif update_arrival.get(count["place"], math.inf) <= now:
            do("place")
        else:
            times = [*arrival.values(), *update_arrival.values(), squares_arrival]
            now = min(time for time in times if time > now)
    return order


class Place:
    def __init__(self, index):
        line = index >> 1 & 3
        self.side = index & 1
        self.upper_line = line >> 1
        self.inner = (line == 1) | (line == 2)


def shards(grad, momentum, placement):
    local_count, row_count, columns = grad.shape
    group_count = lax.axis_size("expert")
    routes = Routes(lax.axis_size("dp"))
    my_group = lax.axis_index("expert")
    my_place = Place(lax.axis_index("dp"))

    slot_ids = lax.iota(jnp.int32, local_count)
    moves = placement.reshape(group_count, local_count)

    def route(group, target):
        row = lax.dynamic_index_in_dim(moves, group, keepdims=False)
        chosen = row // local_count == target
        old_slot = jnp.sum(jnp.where(chosen, slot_ids, 0))
        new_slot = jnp.sum(jnp.where(chosen, row % local_count, 0))
        return old_slot, new_slot

    places = jnp.array(block_places(columns), jnp.int32) * BLOCK
    quarter = places.shape[0] // 4
    quarters = places.reshape(4, quarter, 2)
    order = jnp.stack(
        [my_place.side, 1 - my_place.side, 2 + my_place.upper_line, 3 - my_place.upper_line]
    )
    my_places = jnp.take(quarters, order, axis=0).reshape(4 * quarter, 2).T

    uppers = jnp.stack([my_place.side, my_place.upper_line])

    distances = list(range(group_count - 1, -1, -1))
    momentum_new = None
    update = None
    factors = None
    moved, partial_squares, chains, got, leaving = {}, {}, {}, {}, {}
    front = ()

    def follow(*values):
        return lax.optimization_barrier((values, front))[0]

    for action, which in plan(group_count):
        if action == "hop":
            e, kind, name = which
            needs = kind.hops[name][1]
            arrived = dict(zip(needs, follow(*[got[e, kind][need] for need in needs])))
            (value,) = follow(chains[e, kind].value(name, arrived))
            got[e, kind][name] = send(value, getattr(routes, kind.hops[name][0]))
            front = (value,)
        elif action == "momentum":
            old_slot, _ = route(my_group, my_group ^ distances[which])
            (old_slot,) = follow(old_slot.reshape(1))
            momentum_new, moved[which], sums = momentum_step(
                old_slot, grad, momentum, momentum_new
            )
            partial_squares[which] = jnp.sum(sums)
            front = (sums,)
        elif action == "gram":
            (rows,) = follow(moved[which])
            parts = gram_step(uppers, rows)
            chains[which, SideFirst] = SideFirst(routes, my_place, *parts[:2])
            chains[which, LineFirst] = LineFirst(routes, my_place, *parts[2:])
            got[which, SideFirst], got[which, LineFirst] = {}, {}
            front = tuple(parts[3:])
        elif action == "swaps":
            squares = jnp.stack([partial_squares[e] for e in range(group_count)])
            for pairs in routes.swaps:
                squares = squares + send(squares, pairs)
            factors = 0.5 * math.sqrt(columns) / jnp.sqrt(squares + 1e-06)
        elif action == "update":
            pieces = chains[which, SideFirst].pieces(got[which, SideFirst])
            pieces += chains[which, LineFirst].pieces(got[which, LineFirst])
            pieces = follow(*pieces)
            new_slot = route(my_group ^ distances[which], my_group)[1].reshape(1)
            factor = factors[which].reshape(1)
            rows = moved[which]
            if distances[which] == 0:
                update = update_step(
                    new_slot, my_places, factor, rows, pieces, update, local_count
                )
            else:
                here = jnp.zeros((1,), jnp.int32)
                mine = update_step(here, my_places, factor, rows, pieces)
                pairs = [(g, g ^ distances[which]) for g in range(group_count)]
                leaving[which] = new_slot, lax.ppermute(mine, "expert", pairs)
                front = (mine,)
        else:
            new_slot, arrived = leaving[which]
            (new_slot,) = follow(new_slot)
            update = place_step(new_slot, arrived, update, local_count)
            front = (update,)
    return momentum_new, update


def solution(mesh):
    return jax.shard_map(
        shards,
        mesh=mesh,
        in_specs=(P("expert", "dp", None), P("expert", "dp", None), P()),
        out_specs=(P("expert", "dp", None), P("expert", "dp", None)),
        check_vma=False,
    )
```

```python
import functools
import math

import jax
import jax.numpy as jnp
from jax import lax
from jax.experimental import pallas as pl
from jax.experimental.pallas import tpu as pltpu
from jax.sharding import PartitionSpec as P

D = 7168
BLOCK = 256
STRIP = 512
VMEM_BYTES = 56 * 2**20
SMALL_COST = pl.CostEstimate(flops=2**20, bytes_accessed=2**10, transcendentals=0)


def row_block(rows, most):
    for size in range(most, 15, -16):
        if rows % size == 0:
            return size
    return rows


def momentum_kernel(order_ref, grad_ref, momentum_ref, *refs):
    new_ref, moved_ref, squares_ref = refs[-3:]
    new = 0.95 * momentum_ref[0] + grad_ref[0].astype(jnp.float32)
    new_ref[0] = new
    moved = new.astype(jnp.bfloat16)
    moved_ref[...] = moved
    values = moved.astype(jnp.float32)
    rows, columns = values.shape
    partial_sum = jnp.sum((values * values).reshape(rows // 8, 8, columns), axis=0)

    @pl.when(pl.program_id(0) == 0)
    def _():
        squares_ref[...] = partial_sum

    @pl.when(pl.program_id(0) > 0)
    def _():
        squares_ref[...] += partial_sum


def momentum_step(source, grad, momentum, earlier):
    local_count, rows, columns = grad.shape
    step = row_block(rows, 128)
    spot = pl.BlockSpec((1, step, columns), lambda r, order: (order[0], r, 0))
    in_specs = [spot, spot]
    operands = [source, grad, momentum]
    aliases = {}
    if earlier is not None:
        in_specs.append(pl.BlockSpec(memory_space=pl.ANY))
        operands.append(earlier)
        aliases = {3: 0}
    return pl.pallas_call(
        momentum_kernel,
        grid_spec=pltpu.PrefetchScalarGridSpec(
            num_scalar_prefetch=1,
            grid=(rows // step,),
            in_specs=in_specs,
            out_specs=[
                spot,
                pl.BlockSpec((step, columns), lambda r, order: (r, 0)),
                pl.BlockSpec((8, columns), lambda r, order: (0, 0)),
            ],
        ),
        out_shape=[
            jax.ShapeDtypeStruct(momentum.shape, jnp.float32),
            jax.ShapeDtypeStruct((rows, columns), jnp.bfloat16),
            jax.ShapeDtypeStruct((8, columns), jnp.float32),
        ],
        input_output_aliases=aliases,
        compiler_params=pltpu.CompilerParams(vmem_limit_bytes=VMEM_BYTES),
        cost_estimate=SMALL_COST,
        name="momentum",
    )(*operands)


def block_places(columns):
    count = columns // BLOCK
    return [(i, j) for i in range(count) for j in range(i, count)]


def gram_kernel(upper_ref, rows_ref, *refs):
    outputs, halves, sems = refs[:4], refs[4:6], refs[6]
    columns = rows_ref.shape[1]
    count = columns // BLOCK
    quarter = halves[0].shape[1]
    copies = []
    place = 0
    for i in range(count):
        start = i * BLOCK
        strip = jnp.dot(
            rows_ref[:, start : start + BLOCK].T,
            rows_ref[:, start:],
            preferred_element_type=jnp.float32,
        ).astype(jnp.bfloat16)
        for j in range(count - i):
            half, inside = divmod(place, 2 * quarter)
            part, slot = divmod(inside, quarter)
            halves[half][part, slot] = strip[:, j * BLOCK : (j + 1) * BLOCK]
            place += 1
            if place % (2 * quarter) == 0:
                upper = upper_ref[half]
                for given in range(2):
                    number = 2 * half + given
                    source = upper if given == 0 else 1 - upper
                    copy = pltpu.make_async_copy(
                        halves[half].at[source], outputs[number], sems.at[number]
                    )
                    copy.start()
                    copies.append(copy)
    for copy in copies:
        copy.wait()


def gram_step(uppers, moved):
    rows, columns = moved.shape
    quarter = len(block_places(columns)) // 4
    part = jax.ShapeDtypeStruct((quarter, BLOCK, BLOCK), jnp.bfloat16)
    return pl.pallas_call(
        gram_kernel,
        in_specs=[
            pl.BlockSpec(memory_space=pltpu.SMEM),
            pl.BlockSpec(memory_space=pltpu.VMEM),
        ],
        out_specs=[pl.BlockSpec(memory_space=pl.ANY)] * 4,
        out_shape=[part] * 4,
        scratch_shapes=[
            pltpu.VMEM((2, quarter, BLOCK, BLOCK), jnp.bfloat16),
            pltpu.VMEM((2, quarter, BLOCK, BLOCK), jnp.bfloat16),
            pltpu.SemaphoreType.DMA((4,)),
        ],
        compiler_params=pltpu.CompilerParams(vmem_limit_bytes=VMEM_BYTES),
        cost_estimate=SMALL_COST,
        name="gram",
    )(uppers, moved)


def update_kernel(slot_ref, place_ref, factor_ref, rows_ref, *refs):
    pieces = refs[:4]
    out_ref, gram_ref, normal_ref, product_ref = refs[-4:]
    piece_blocks = pieces[0].shape[0]

    @pl.when(pl.program_id(0) == 0)
    def _():
        for number, piece in enumerate(pieces):
            for block in range(piece_blocks):
                index = number * piece_blocks + block
                row = pl.multiple_of(place_ref[0, index], BLOCK)
                column = pl.multiple_of(place_ref[1, index], BLOCK)
                value = piece[block]
                gram_ref[pl.ds(row, BLOCK), pl.ds(column, BLOCK)] = value
                gram_ref[pl.ds(column, BLOCK), pl.ds(row, BLOCK)] = value.T

    factor = factor_ref[0]
    factor_squared = factor * factor
    normal_ref[...] = (rows_ref[...].astype(jnp.float32) * factor).astype(jnp.bfloat16)
    columns = gram_ref.shape[0]
    strips = [slice(start, start + STRIP) for start in range(0, columns, STRIP)]
    for here in strips:
        product = jnp.dot(
            normal_ref[...], gram_ref[:, here], preferred_element_type=jnp.float32
        )
        product_ref[:, here] = (product * factor_squared).astype(jnp.bfloat16)
    for here in strips:
        second = jnp.dot(
            product_ref[...], gram_ref[:, here], preferred_element_type=jnp.float32
        )
        orthogonal = (
            3.4445 * normal_ref[:, here].astype(jnp.float32)
            - 4.775 * product_ref[:, here].astype(jnp.float32)
            + 2.0315 * (second * factor_squared)
        )
        out_ref[0, :, here] = (orthogonal * math.sqrt(D)).astype(jnp.bfloat16)


def update_step(slot, places, factor, moved, pieces, earlier=None, count=1):
    rows, columns = moved.shape
    step = rows // 2 if rows % 32 == 0 and rows >= 512 else rows
    whole = pl.BlockSpec(pieces[0].shape, lambda r, *_: (0, 0, 0))
    in_specs = [
        pl.BlockSpec(memory_space=pltpu.SMEM),
        pl.BlockSpec((step, columns), lambda r, *_: (r, 0)),
    ] + [whole] * 4
    operands = [slot, places, factor, moved, *pieces]
    aliases = {}
    if earlier is not None:
        in_specs.append(pl.BlockSpec(memory_space=pl.ANY))
        operands.append(earlier)
        aliases = {8: 0}
    return pl.pallas_call(
        update_kernel,
        grid_spec=pltpu.PrefetchScalarGridSpec(
            num_scalar_prefetch=2,
            grid=(rows // step,),
            in_specs=in_specs,
            out_specs=pl.BlockSpec((1, step, columns), lambda r, slot, *_: (slot[0], r, 0)),
            scratch_shapes=[
                pltpu.VMEM((columns, columns), jnp.bfloat16),
                pltpu.VMEM((step, columns), jnp.bfloat16),
                pltpu.VMEM((step, columns), jnp.bfloat16),
            ],
        ),
        out_shape=jax.ShapeDtypeStruct((count, rows, columns), jnp.bfloat16),
        input_output_aliases=aliases,
        compiler_params=pltpu.CompilerParams(vmem_limit_bytes=VMEM_BYTES),
        cost_estimate=SMALL_COST,
        name="update",
    )(*operands)


def place_kernel(cuts, slot_ref, *refs):
    for number in range(cuts):

        @pl.when(pl.program_id(0) == number)
        def _():
            refs[-1][...] = refs[number][...]


def place_step(slot, arrived, earlier, count):
    cuts = len(arrived)
    _, rows, columns = arrived[0].shape
    in_specs = [pl.BlockSpec((1, rows, columns), lambda r, slot: (0, 0, 0))] * cuts
    operands = [slot, *arrived]
    aliases = {}
    if earlier is not None:
        in_specs.append(pl.BlockSpec(memory_space=pl.ANY))
        operands.append(earlier)
        aliases = {cuts + 1: 0}
    return pl.pallas_call(
        functools.partial(place_kernel, cuts),
        grid_spec=pltpu.PrefetchScalarGridSpec(
            num_scalar_prefetch=1,
            grid=(cuts,),
            in_specs=in_specs,
            out_specs=pl.BlockSpec((1, rows, columns), lambda r, slot: (slot[0], r, 0)),
        ),
        out_shape=jax.ShapeDtypeStruct((count, cuts * rows, columns), jnp.bfloat16),
        input_output_aliases=aliases,
        compiler_params=pltpu.CompilerParams(vmem_limit_bytes=VMEM_BYTES),
        cost_estimate=SMALL_COST,
        name="place",
    )(*operands)


def add_up(mine, arrived):
    return (mine.astype(jnp.float32) + arrived.astype(jnp.float32)).astype(jnp.bfloat16)


class Routes:
    def __init__(self, dp_count):
        everyone = range(dp_count)
        line = lambda i: i >> 1 & 3
        self.side = [(i, i ^ 1) for i in everyone]
        self.inner_side = [(i, i ^ 1) for i in everyone if line(i) in (1, 2)]
        self.inward = [(i, i + 2) for i in everyone if line(i) == 0]
        self.inward += [(i, i - 2) for i in everyone if line(i) == 3]
        self.outward = [(b, a) for a, b in self.inward]
        self.middle = [(i, i + 2) for i in everyone if line(i) == 1]
        self.middle += [(i, i - 2) for i in everyone if line(i) == 2]
        self.swaps = [[(i, i ^ 1 << bit) for i in everyone] for bit in range(dp_count.bit_length() - 1)]
        self.far = []
        distance = 8
        while distance < dp_count:
            self.far.append([(i, i ^ distance) for i in everyone])
            distance *= 2


def send(value, pairs):
    return lax.ppermute(value, "dp", pairs)


class SideFirst:
    hops = {
        "side": ("side", (), 0),
        "in": ("inward", ("side",), 1),
        "middle": ("middle", ("in",), 1),
        "out": ("outward", ("middle",), 1),
        "gather": ("side", ("out",), 1),
    }

    def __init__(self, routes, place, kept, given):
        self.routes, self.inner = routes, place.inner
        self.kept, self.given = kept, given

    def value(self, hop, got):
        if hop == "side":
            return self.given
        if hop == "in":
            self.total = add_up(self.kept, got["side"])
        elif hop == "middle":
            self.total = add_up(self.total, got["in"])
        elif hop == "out":
            self.total = add_up(self.total, got["middle"])
            for pairs in self.routes.far:
                self.total = add_up(self.total, send(self.total, pairs))
        else:
            self.total = jnp.where(self.inner, self.total, got["out"])
        return self.total

    def pieces(self, got):
        return self.total, got["gather"]


class LineFirst:
    hops = {
        "in given": ("inward", (), 0),
        "in kept": ("inward", (), 0),
        "middle": ("middle", ("in given",), 1),
        "side": ("inner_side", ("in kept", "middle"), 2),
        "middle back": ("middle", ("side",), 1),
        "out": ("outward", ("side",), 0),
        "out other": ("outward", ("middle back",), 0),
    }

    def __init__(self, routes, place, kept, given):
        self.routes, self.inner = routes, place.inner
        self.kept, self.given = kept, given
        self.total = None

    def value(self, hop, got):
        if hop == "in given":
            return self.given
        if hop == "in kept":
            return self.kept
        if hop == "middle":
            return add_up(self.given, got["in given"])
        if hop == "side":
            self.kept = add_up(add_up(self.kept, got["in kept"]), got["middle"])
            return self.kept
        if hop == "out other":
            return got["middle back"]
        if self.total is None:
            self.total = add_up(self.kept, got["side"])
            for pairs in self.routes.far:
                self.total = add_up(self.total, send(self.total, pairs))
        return self.total

    def pieces(self, got):
        return (
            jnp.where(self.inner, self.total, got["out"]),
            jnp.where(self.inner, got["middle back"], got["out other"]),
        )


def plan(experts, swap_count):
    transfer, latency, issue, pass_over = 23.3, 5.0, 1.6, 1.6
    takes = {"momentum": 12.0, "gram": 9.0, "update": 20.0, "place": 5.0}
    near, far = 20.0, 78.0
    hops = {}
    for expert in range(experts):
        for kind in (LineFirst, SideFirst):
            for name, (link, needs, passes) in kind.hops.items():
                needed = [(expert, kind, need) for need in needs]
                hops[expert, kind, name] = (link.replace("inner_", ""), needed, passes)
    last_hops = {}

    def length(hop):
        if hop not in last_hops:
            later = [length(h) for h in hops if hop in hops[h][1]]
            last_hops[hop] = 1 + max(later, default=0)
        return last_hops[hop]

    first_choice = sorted(hops, key=lambda hop: (hop[0], -length(hop)))
    order = []
    now = 0.0
    count = dict.fromkeys(takes, 0)
    arrival = {}
    queues = {}
    update_arrival = {}
    far_free = 0.0

    taken = set()
    swapped = 0
    swap_arrival = math.inf

    def put(action, which):
        arrived = [hop for hop in arrival if arrival[hop] <= now and hop not in taken]
        taken.update(arrived)
        order.append((action, which, arrived))

    def do(kernel):
        nonlocal now
        put(kernel, count[kernel])
        count[kernel] += 1
        now += takes[kernel]

    def next_hop():
        for hop in first_choice:
            link, needed, _ = hops[hop]
            queued = sum(time > now for time in queues.setdefault(link, []))
            if hop[0] < count["gram"] and hop not in arrival and queued < 2:
                if all(arrival.get(need, math.inf) <= now for need in needed):
                    return hop
        return None

    do("momentum")
    do("gram")
    while count["place"] < experts - 1:
        hop = next_hop()
        updating = count["update"]
        last = updating == experts - 1
        early = count["place"] < experts - 2 or updating == experts
        mine = [h for h in hops if h[0] == updating]
        whole = updating < experts and all(arrival.get(h, math.inf) <= now for h in mine)
        if updating == experts - 2:
            whole = whole and len(arrival) == len(hops)
        squares_in = swap_arrival if swapped == swap_count else math.inf
        if hop is not None:
            link, _, passes = hops[hop]
            put("hop", hop)
            now += issue + passes * pass_over
            queue = queues[link]
            queue.append(max([now + 1, *queue[-1:]]) + transfer)
            arrival[hop] = queue[-1] + latency
        elif count["gram"] < count["momentum"]:
            do("gram")
        elif count["momentum"] < experts:
            do("momentum")
            if count["momentum"] == experts:
                swap_arrival = now
        elif swapped < swap_count and swap_arrival <= now:
            put("swap", swapped)
            now += issue + pass_over
            swapped += 1
            swap_arrival = max([now, *(queue[-1] for queue in queues.values() if queue)]) + latency
        elif whole and squares_in <= now and (not last or count["place"] >= updating - 1):
            do("update")
            if updating < experts - 2:
                far_free = max(now, far_free) + far
                update_arrival[updating] = far_free
            else:
                update_arrival[updating] = now + near
        elif early and update_arrival.get(count["place"], math.inf) <= now:
            do("place")
        else:
            times = [*arrival.values(), *update_arrival.values(), swap_arrival]
            now = min(time for time in times if time > now)
    return order


class Place:
    def __init__(self, index):
        line = index >> 1 & 3
        self.side = index & 1
        self.upper_line = line >> 1
        self.inner = (line == 1) | (line == 2)


def shards(grad, momentum, placement):
    local_count, row_count, columns = grad.shape
    group_count = lax.axis_size("expert")
    routes = Routes(lax.axis_size("dp"))
    my_group = lax.axis_index("expert")
    my_place = Place(lax.axis_index("dp"))

    slot_ids = lax.iota(jnp.int32, local_count)
    moves = placement.reshape(group_count, local_count)

    def route(group, target):
        row = lax.dynamic_index_in_dim(moves, group, keepdims=False)
        chosen = row // local_count == target
        old_slot = jnp.sum(jnp.where(chosen, slot_ids, 0))
        new_slot = jnp.sum(jnp.where(chosen, row % local_count, 0))
        return old_slot, new_slot

    places = jnp.array(block_places(columns), jnp.int32) * BLOCK
    quarter = places.shape[0] // 4
    quarters = places.reshape(4, quarter, 2)
    order = jnp.stack(
        [my_place.side, 1 - my_place.side, 2 + my_place.upper_line, 3 - my_place.upper_line]
    )
    my_places = jnp.take(quarters, order, axis=0).reshape(4 * quarter, 2).T

    uppers = jnp.stack([my_place.side, my_place.upper_line])

    distances = list(range(group_count - 1, -1, -1))
    momentum_new = None
    update = None
    factors, squares, other_squares = None, None, None
    moved, partial_squares, chains, got, leaving = {}, {}, {}, {}, {}
    front = ()

    def follow(*values):
        return lax.optimization_barrier((values, front))[0]

    for action, which, arrived_hops in plan(group_count, len(routes.swaps)):
        taken = follow(*[got[e, kind][name] for e, kind, name in arrived_hops])
        for (e, kind, name), arrival in zip(arrived_hops, taken):
            got[e, kind][name] = arrival
        front = (*front, *taken)
        if action == "hop":
            e, kind, name = which
            needs = kind.hops[name][1]
            arrived = dict(zip(needs, follow(*[got[e, kind][need] for need in needs])))
            (value,) = follow(chains[e, kind].value(name, arrived))
            got[e, kind][name] = send(value, getattr(routes, kind.hops[name][0]))
            front = (value,)
        elif action == "momentum":
            old_slot, _ = route(my_group, my_group ^ distances[which])
            (old_slot,) = follow(old_slot.reshape(1))
            momentum_new, moved[which], sums = momentum_step(
                old_slot, grad, momentum, momentum_new
            )
            partial_squares[which] = jnp.sum(sums)
            front = (sums,)
        elif action == "gram":
            (rows,) = follow(moved[which])
            parts = gram_step(uppers, rows)
            chains[which, SideFirst] = SideFirst(routes, my_place, *parts[:2])
            chains[which, LineFirst] = LineFirst(routes, my_place, *parts[2:])
            got[which, SideFirst], got[which, LineFirst] = {}, {}
            front = tuple(parts[3:])
        elif action == "swap":
            if which == 0:
                squares = jnp.stack([partial_squares[e] for e in range(group_count)])
            else:
                squares = squares + follow(other_squares)[0]
            (squares,) = follow(squares)
            other_squares = send(squares, routes.swaps[which])
            front = (squares,)
        elif action == "update":
            pieces = chains[which, SideFirst].pieces(got[which, SideFirst])
            pieces += chains[which, LineFirst].pieces(got[which, LineFirst])
            pieces = follow(*pieces)
            new_slot = route(my_group ^ distances[which], my_group)[1].reshape(1)
            if which == 0:
                squares = squares + follow(other_squares)[0]
                factors = 0.5 * math.sqrt(columns) / jnp.sqrt(squares + 1e-06)
            factor = factors[which].reshape(1)
            rows = moved[which]
            if distances[which] == 0:
                update = update_step(
                    new_slot, my_places, factor, rows, pieces, update, local_count
                )
                front = (update,)
            else:
                here = jnp.zeros((1,), jnp.int32)
                mine = update_step(here, my_places, factor, rows, pieces)
                pairs = [(g, g ^ distances[which]) for g in range(group_count)]
                cuts = 4 if distances[which] == 1 and row_count % 64 == 0 else 1
                cut_rows = [
                    lax.ppermute(cut, "expert", pairs) for cut in jnp.split(mine, cuts, axis=1)
                ]
                leaving[which] = new_slot, cut_rows
                front = (mine,)
        else:
            new_slot, arrived = leaving[which]
            (new_slot,) = follow(new_slot)
            update = place_step(new_slot, arrived, update, local_count)
            front = (update,)
    return momentum_new, update


def solution(mesh):
    return jax.shard_map(
        shards,
        mesh=mesh,
        in_specs=(P("expert", "dp", None), P("expert", "dp", None), P()),
        out_specs=(P("expert", "dp", None), P("expert", "dp", None)),
        check_vma=False,
    )
```

```python
import functools
import math

import jax
import jax.numpy as jnp
from jax import lax
from jax.experimental import pallas as pl
from jax.experimental.pallas import tpu as pltpu
from jax.sharding import PartitionSpec as P

D = 7168
BLOCK = 256
EXTRA_ROWS = 16
VMEM_BYTES = 56 * 2**20
SMALL_COST = pl.CostEstimate(flops=2**20, bytes_accessed=2**10, transcendentals=0)


def row_block(rows, most):
    for size in range(most, 15, -16):
        if rows % size == 0:
            return size
    return rows


def momentum_kernel(order_ref, grad_ref, momentum_ref, *refs):
    new_ref, moved_ref = refs[-2:]
    new = 0.95 * momentum_ref[0] + grad_ref[0].astype(jnp.float32)
    new_ref[0] = new
    moved_ref[...] = new.astype(jnp.bfloat16)


def momentum_step(source, grad, momentum, earlier):
    local_count, rows, columns = grad.shape
    step = row_block(rows, 128)
    spot = pl.BlockSpec((1, step, columns), lambda r, order: (order[0], r, 0))
    in_specs = [spot, spot]
    operands = [source, grad, momentum]
    aliases = {}
    if earlier is not None:
        in_specs.append(pl.BlockSpec(memory_space=pl.ANY))
        operands.append(earlier)
        aliases = {3: 0}
    return pl.pallas_call(
        momentum_kernel,
        grid_spec=pltpu.PrefetchScalarGridSpec(
            num_scalar_prefetch=1,
            grid=(rows // step,),
            in_specs=in_specs,
            out_specs=[spot, pl.BlockSpec((step, columns), lambda r, order: (r, 0))],
        ),
        out_shape=[
            jax.ShapeDtypeStruct(momentum.shape, jnp.float32),
            jax.ShapeDtypeStruct((rows, columns), jnp.bfloat16),
        ],
        input_output_aliases=aliases,
        compiler_params=pltpu.CompilerParams(vmem_limit_bytes=VMEM_BYTES),
        cost_estimate=SMALL_COST,
        name="momentum",
    )(*operands)


def block_places(columns):
    count = columns // BLOCK
    return [(i, j) for i in range(count) for j in range(i, count)]


def squares_tile(squares, index):
    top = float(jnp.finfo(jnp.bfloat16).max)
    spot = lax.broadcasted_iota(jnp.int32, (EXTRA_ROWS, BLOCK), 0) * BLOCK
    spot += lax.broadcasted_iota(jnp.int32, (EXTRA_ROWS, BLOCK), 1)
    tile = jnp.zeros((EXTRA_ROWS, BLOCK), jnp.float32)
    rest = squares
    for number in range(3):
        piece = jnp.minimum(rest, top).astype(jnp.bfloat16).astype(jnp.float32)
        tile = jnp.where(spot == 3 * index + number, piece, tile)
        rest = rest - piece
    return tile.astype(jnp.bfloat16)


def gram_kernel(where_ref, rows_ref, *refs):
    outputs, halves, sems = refs[:4], refs[4:6], refs[6]
    columns = rows_ref.shape[1]
    count = columns // BLOCK
    quarter = halves[0].shape[1] // BLOCK
    diagonal = lax.broadcasted_iota(jnp.int32, (BLOCK, BLOCK), 0) == lax.broadcasted_iota(
        jnp.int32, (BLOCK, BLOCK), 1
    )
    on_diagonal = jnp.zeros((BLOCK, BLOCK), jnp.float32)
    copies = []

    def send_out(half):
        upper = where_ref[half]
        for given in range(2):
            number = 2 * half + given
            source = upper if given == 0 else 1 - upper
            copy = pltpu.make_async_copy(
                halves[half].at[source], outputs[number], sems.at[number]
            )
            copy.start()
            copies.append(copy)

    place = 0
    for i in range(count):
        start = i * BLOCK
        strip = jnp.dot(
            rows_ref[:, start : start + BLOCK].T,
            rows_ref[:, start:],
            preferred_element_type=jnp.float32,
        )
        on_diagonal += jnp.where(diagonal, strip[:, :BLOCK], 0.0)
        for j in range(count - i):
            half, inside = divmod(place, 2 * quarter)
            part, slot = divmod(inside, quarter)
            halves[half][part, slot * BLOCK : (slot + 1) * BLOCK] = strip[
                :, j * BLOCK : (j + 1) * BLOCK
            ].astype(jnp.bfloat16)
            place += 1
            if place == 2 * quarter:
                send_out(0)
    squares = jnp.sum(on_diagonal, keepdims=True)
    halves[1][0, quarter * BLOCK :] = squares_tile(squares, where_ref[2])
    halves[1][1, quarter * BLOCK :] = jnp.zeros((EXTRA_ROWS, BLOCK), jnp.bfloat16)
    send_out(1)
    for copy in copies:
        copy.wait()


def gram_step(where, moved):
    columns = moved.shape[1]
    quarter = len(block_places(columns)) // 4 * BLOCK
    shapes = [(quarter, BLOCK), (quarter + EXTRA_ROWS, BLOCK)]
    return pl.pallas_call(
        gram_kernel,
        in_specs=[
            pl.BlockSpec(memory_space=pltpu.SMEM),
            pl.BlockSpec(memory_space=pltpu.VMEM),
        ],
        out_specs=[pl.BlockSpec(memory_space=pl.ANY)] * 4,
        out_shape=[jax.ShapeDtypeStruct(shapes[n // 2], jnp.bfloat16) for n in range(4)],
        scratch_shapes=[pltpu.VMEM((2, *shape), jnp.bfloat16) for shape in shapes]
        + [pltpu.SemaphoreType.DMA((4,))],
        compiler_params=pltpu.CompilerParams(vmem_limit_bytes=VMEM_BYTES),
        cost_estimate=SMALL_COST,
        name="gram",
    )(where, moved)


def times_gram(left_ref, gram_ref, j):
    start = j * BLOCK
    stop = start + BLOCK
    total = lax.dot_general(
        left_ref[:, start:],
        gram_ref[start:stop, start:],
        (((1,), (1,)), ((), ())),
        preferred_element_type=jnp.float32,
    )
    if j > 0:
        total += jnp.dot(
            left_ref[:, :start], gram_ref[:start, start:stop], preferred_element_type=jnp.float32
        )
    return total


def update_kernel(slot_ref, place_ref, rows_ref, *refs):
    pieces = refs[:4]
    out_ref, gram_ref, normal_ref, product_ref = refs[-4:]
    columns = gram_ref.shape[0]
    count = columns // BLOCK
    piece_blocks = pieces[0].shape[0] // BLOCK
    squares = sum(
        jnp.sum(piece[piece_blocks * BLOCK :].astype(jnp.float32), keepdims=True)
        for piece in pieces[2:]
    )
    factor = 0.5 * math.sqrt(columns) / jnp.sqrt(squares + 1e-06)
    factor_squared = factor * factor

    @pl.when(pl.program_id(0) == 0)
    def _():
        finite = squares < math.inf
        for number, piece in enumerate(pieces):
            for block in range(piece_blocks):
                index = number * piece_blocks + block
                row = pl.multiple_of(place_ref[0, index], BLOCK)
                column = pl.multiple_of(place_ref[1, index], BLOCK)
                value = piece[block * BLOCK : (block + 1) * BLOCK]
                gram_ref[pl.ds(row, BLOCK), pl.ds(column, BLOCK)] = jnp.where(
                    finite, value, jnp.zeros_like(value)
                )

    normal_ref[...] = (rows_ref[...].astype(jnp.float32) * factor).astype(jnp.bfloat16)
    for j in range(count):
        product = times_gram(normal_ref, gram_ref, j) * factor_squared
        product_ref[:, j * BLOCK : (j + 1) * BLOCK] = product.astype(jnp.bfloat16)
    for j in range(count):
        here = slice(j * BLOCK, (j + 1) * BLOCK)
        second = times_gram(product_ref, gram_ref, j) * factor_squared
        orthogonal = (
            3.4445 * normal_ref[:, here].astype(jnp.float32)
            - 4.775 * product_ref[:, here].astype(jnp.float32)
            + 2.0315 * second
        )
        out_ref[0, :, here] = (orthogonal * math.sqrt(D)).astype(jnp.bfloat16)


def update_step(slot, places, moved, pieces, earlier=None, count=1):
    rows, columns = moved.shape
    step = rows // 2 if rows % 32 == 0 and rows >= 512 else rows
    in_specs = [pl.BlockSpec((step, columns), lambda r, *_: (r, 0))]
    in_specs += [pl.BlockSpec(piece.shape, lambda r, *_: (0, 0)) for piece in pieces]
    operands = [slot, places, moved, *pieces]
    aliases = {}
    if earlier is not None:
        in_specs.append(pl.BlockSpec(memory_space=pl.ANY))
        operands.append(earlier)
        aliases = {7: 0}
    return pl.pallas_call(
        update_kernel,
        grid_spec=pltpu.PrefetchScalarGridSpec(
            num_scalar_prefetch=2,
            grid=(rows // step,),
            in_specs=in_specs,
            out_specs=pl.BlockSpec((1, step, columns), lambda r, slot, *_: (slot[0], r, 0)),
            scratch_shapes=[
                pltpu.VMEM((columns, columns), jnp.bfloat16),
                pltpu.VMEM((step, columns), jnp.bfloat16),
                pltpu.VMEM((step, columns), jnp.bfloat16),
            ],
        ),
        out_shape=jax.ShapeDtypeStruct((count, rows, columns), jnp.bfloat16),
        input_output_aliases=aliases,
        compiler_params=pltpu.CompilerParams(vmem_limit_bytes=VMEM_BYTES),
        cost_estimate=SMALL_COST,
        name="update",
    )(*operands)


def place_kernel(cuts, slot_ref, *refs):
    for number in range(cuts):

        @pl.when(pl.program_id(0) == number)
        def _():
            refs[-1][...] = refs[number][...]


def place_step(slot, arrived, earlier, count):
    cuts = len(arrived)
    _, rows, columns = arrived[0].shape
    in_specs = [pl.BlockSpec((1, rows, columns), lambda r, slot: (0, 0, 0))] * cuts
    operands = [slot, *arrived]
    aliases = {}
    if earlier is not None:
        in_specs.append(pl.BlockSpec(memory_space=pl.ANY))
        operands.append(earlier)
        aliases = {cuts + 1: 0}
    return pl.pallas_call(
        functools.partial(place_kernel, cuts),
        grid_spec=pltpu.PrefetchScalarGridSpec(
            num_scalar_prefetch=1,
            grid=(cuts,),
            in_specs=in_specs,
            out_specs=pl.BlockSpec((1, rows, columns), lambda r, slot: (slot[0], r, 0)),
        ),
        out_shape=jax.ShapeDtypeStruct((count, cuts * rows, columns), jnp.bfloat16),
        input_output_aliases=aliases,
        compiler_params=pltpu.CompilerParams(vmem_limit_bytes=VMEM_BYTES),
        cost_estimate=SMALL_COST,
        name="place",
    )(*operands)


def add_up(mine, arrived):
    return (mine.astype(jnp.float32) + arrived.astype(jnp.float32)).astype(jnp.bfloat16)


class Routes:
    def __init__(self, dp_count):
        everyone = range(dp_count)
        line = lambda i: i >> 1 & 3
        self.side = [(i, i ^ 1) for i in everyone]
        self.inner_side = [(i, i ^ 1) for i in everyone if line(i) in (1, 2)]
        self.inward = [(i, i + 2) for i in everyone if line(i) == 0]
        self.inward += [(i, i - 2) for i in everyone if line(i) == 3]
        self.outward = [(b, a) for a, b in self.inward]
        self.middle = [(i, i + 2) for i in everyone if line(i) == 1]
        self.middle += [(i, i - 2) for i in everyone if line(i) == 2]
        self.far = []
        distance = 8
        while distance < dp_count:
            self.far.append([(i, i ^ distance) for i in everyone])
            distance *= 2


def send(value, pairs):
    return lax.ppermute(value, "dp", pairs)


class SideFirst:
    hops = {
        "side": ("side", (), 0),
        "in": ("inward", ("side",), 1),
        "middle": ("middle", ("in",), 1),
        "out": ("outward", ("middle",), 1),
        "gather": ("side", ("out",), 1),
    }

    def __init__(self, routes, place, kept, given):
        self.routes, self.inner = routes, place.inner
        self.kept, self.given = kept, given

    def value(self, hop, got):
        if hop == "side":
            return self.given
        if hop == "in":
            self.total = add_up(self.kept, got["side"])
        elif hop == "middle":
            self.total = add_up(self.total, got["in"])
        elif hop == "out":
            self.total = add_up(self.total, got["middle"])
            for pairs in self.routes.far:
                self.total = add_up(self.total, send(self.total, pairs))
        else:
            self.total = jnp.where(self.inner, self.total, got["out"])
        return self.total

    def pieces(self, got):
        return self.total, got["gather"]


class LineFirst:
    hops = {
        "in given": ("inward", (), 0),
        "in kept": ("inward", (), 0),
        "middle": ("middle", ("in given",), 1),
        "side": ("inner_side", ("in kept", "middle"), 2),
        "middle back": ("middle", ("side",), 1),
        "out": ("outward", ("side",), 0),
        "out other": ("outward", ("middle back",), 0),
    }

    def __init__(self, routes, place, kept, given):
        self.routes, self.inner = routes, place.inner
        self.kept, self.given = kept, given
        self.total = None

    def value(self, hop, got):
        if hop == "in given":
            return self.given
        if hop == "in kept":
            return self.kept
        if hop == "middle":
            return add_up(self.given, got["in given"])
        if hop == "side":
            self.kept = add_up(add_up(self.kept, got["in kept"]), got["middle"])
            return self.kept
        if hop == "out other":
            return got["middle back"]
        if self.total is None:
            self.total = add_up(self.kept, got["side"])
            for pairs in self.routes.far:
                self.total = add_up(self.total, send(self.total, pairs))
        return self.total

    def pieces(self, got):
        return (
            jnp.where(self.inner, self.total, got["out"]),
            jnp.where(self.inner, got["middle back"], got["out other"]),
        )


def plan(experts):
    transfer, latency, issue, pass_over = 23.3, 3.0, 2.5, 1.8
    takes = {"momentum": 12.0, "gram": 9.0, "update": 28.0, "place": 5.0}
    near, far = 12.0, 78.0
    deepest, patience, backlog = 4, 4.0, 10.0
    hops = {}
    for expert in range(experts):
        for kind in (LineFirst, SideFirst):
            for name, (link, needs, passes) in kind.hops.items():
                needed = [(expert, kind, need) for need in needs]
                hops[expert, kind, name] = (link.replace("inner_", ""), needed, passes)
    lengths = {}

    def length(hop):
        if hop not in lengths:
            later = [length(h) for h in hops if hop in hops[h][1]]
            lengths[hop] = 1 + max(later, default=0)
        return lengths[hop]

    def rank(hop):
        return hop[0] - length(hop) - (0.5 if hop[1] is SideFirst else 0), hop[0]

    first_choice = sorted(hops, key=rank)
    order = []
    now = 0.0
    count = dict.fromkeys(takes, 0)
    arrival = {}
    queues = {link: [] for link, _, _ in hops.values()}
    update_arrival = {}
    far_free = 0.0
    taken = set()

    def put(action, which):
        arrived = [hop for hop in arrival if arrival[hop] <= now and hop not in taken]
        taken.update(arrived)
        order.append((action, which, arrived))

    def do(kernel):
        nonlocal now
        put(kernel, count[kernel])
        count[kernel] += 1
        now += takes[kernel]

    def next_hop():
        for hop in first_choice:
            link, needed, _ = hops[hop]
            queued = sum(time > now for time in queues[link])
            if hop[0] < count["gram"] and hop not in arrival and queued < deepest:
                if all(arrival.get(need, math.inf) <= now for need in needed):
                    return hop
        return None

    do("momentum")
    do("gram")
    while count["place"] < experts - 1:
        updating = count["update"]
        last = updating == experts - 1
        early = count["place"] < experts - 2 or updating == experts
        mine = [h for h in hops if h[0] == updating]
        whole = updating < experts and all(arrival.get(h, math.inf) <= now for h in mine)
        if updating == experts - 2:
            whole = whole and len(arrival) == len(hops)
        if last:
            whole = whole and count["place"] >= updating - 1
        coming = min((time for time in arrival.values() if time > now), default=math.inf)
        ahead = min(max([0.0] + [time - now for time in queue]) for queue in queues.values())
        free = last or coming - now >= patience or ahead >= backlog
        hop = next_hop()
        if hop is not None:
            link, _, passes = hops[hop]
            put("hop", hop)
            now += issue + passes * pass_over
            queue = queues[link]
            queue.append(max([now + 1, *queue[-1:]]) + transfer)
            arrival[hop] = queue[-1] + latency
        elif count["gram"] < count["momentum"]:
            do("gram")
        elif count["momentum"] < experts:
            do("momentum")
        elif whole and free:
            do("update")
            if updating < experts - 2:
                far_free = max(now, far_free) + far
                update_arrival[updating] = far_free
            else:
                update_arrival[updating] = now + near
        elif early and update_arrival.get(count["place"], math.inf) <= now:
            do("place")
        else:
            times = [*arrival.values(), *update_arrival.values()]
            now = min(time for time in times if time > now)
    return order


class Place:
    def __init__(self, index):
        line = index >> 1 & 3
        self.side = index & 1
        self.upper_line = line >> 1
        self.inner = (line == 1) | (line == 2)


def shards(grad, momentum, placement):
    local_count, row_count, columns = grad.shape
    group_count = lax.axis_size("expert")
    routes = Routes(lax.axis_size("dp"))
    my_group = lax.axis_index("expert")
    my_place = Place(lax.axis_index("dp"))

    slot_ids = lax.iota(jnp.int32, local_count)
    moves = placement.reshape(group_count, local_count)

    def route(group, target):
        row = lax.dynamic_index_in_dim(moves, group, keepdims=False)
        chosen = row // local_count == target
        old_slot = jnp.sum(jnp.where(chosen, slot_ids, 0))
        new_slot = jnp.sum(jnp.where(chosen, row % local_count, 0))
        return old_slot, new_slot

    places = jnp.array(block_places(columns), jnp.int32) * BLOCK
    quarter = places.shape[0] // 4
    quarters = places.reshape(4, quarter, 2)
    order = jnp.stack(
        [my_place.side, 1 - my_place.side, 2 + my_place.upper_line, 3 - my_place.upper_line]
    )
    my_places = jnp.take(quarters, order, axis=0).reshape(4 * quarter, 2).T

    where = jnp.stack([my_place.side, my_place.upper_line, lax.axis_index("dp")])

    distances = list(range(group_count - 1, -1, -1))
    momentum_new = None
    update = None
    moved, chains, got, leaving = {}, {}, {}, {}
    front = ()

    def follow(*values):
        return lax.optimization_barrier((values, front))[0]

    for action, which, arrived_hops in plan(group_count):
        taken = follow(*[got[e, kind][name] for e, kind, name in arrived_hops])
        for (e, kind, name), arrival in zip(arrived_hops, taken):
            got[e, kind][name] = arrival
        front = (*front, *taken)
        if action == "hop":
            e, kind, name = which
            needs = kind.hops[name][1]
            arrived = dict(zip(needs, follow(*[got[e, kind][need] for need in needs])))
            (value,) = follow(chains[e, kind].value(name, arrived))
            got[e, kind][name] = send(value, getattr(routes, kind.hops[name][0]))
            front = (value,)
        elif action == "momentum":
            old_slot, _ = route(my_group, my_group ^ distances[which])
            (old_slot,) = follow(old_slot.reshape(1))
            momentum_new, moved[which] = momentum_step(old_slot, grad, momentum, momentum_new)
            front = (moved[which],)
        elif action == "gram":
            (rows,) = follow(moved[which])
            parts = gram_step(where, rows)
            chains[which, SideFirst] = SideFirst(routes, my_place, *parts[:2])
            chains[which, LineFirst] = LineFirst(routes, my_place, *parts[2:])
            got[which, SideFirst], got[which, LineFirst] = {}, {}
            front = tuple(parts[3:])
        elif action == "update":
            pieces = chains[which, SideFirst].pieces(got[which, SideFirst])
            pieces += chains[which, LineFirst].pieces(got[which, LineFirst])
            pieces = follow(*pieces)
            new_slot = route(my_group ^ distances[which], my_group)[1].reshape(1)
            rows = moved[which]
            if distances[which] == 0:
                update = update_step(
                    new_slot, my_places, rows, pieces, update, local_count
                )
                front = (update,)
            else:
                here = jnp.zeros((1,), jnp.int32)
                mine = update_step(here, my_places, rows, pieces)
                pairs = [(g, g ^ distances[which]) for g in range(group_count)]
                cuts = 4 if distances[which] == 1 and row_count % 64 == 0 else 1
                cut_rows = [
                    lax.ppermute(cut, "expert", pairs) for cut in jnp.split(mine, cuts, axis=1)
                ]
                leaving[which] = new_slot, cut_rows
                front = (mine,)
        else:
            new_slot, arrived = leaving[which]
            (new_slot,) = follow(new_slot)
            update = place_step(new_slot, arrived, update, local_count)
            front = (update,)
    return momentum_new, update


def solution(mesh):
    return jax.shard_map(
        shards,
        mesh=mesh,
        in_specs=(P("expert", "dp", None), P("expert", "dp", None), P()),
        out_specs=(P("expert", "dp", None), P("expert", "dp", None)),
        check_vma=False,
    )
```

```python
import functools
import math

import jax
import jax.numpy as jnp
from jax import lax
from jax.experimental import pallas as pl
from jax.experimental.pallas import tpu as pltpu
from jax.sharding import PartitionSpec as P

D = 7168
BLOCK = 256
EXTRA_ROWS = 16
VMEM_BYTES = 56 * 2**20
SMALL_COST = pl.CostEstimate(flops=2**20, bytes_accessed=2**10, transcendentals=0)


def row_block(rows, most):
    for size in range(most, 15, -16):
        if rows % size == 0:
            return size
    return rows


def momentum_kernel(order_ref, grad_ref, momentum_ref, *refs):
    new_ref, moved_ref = refs[-2:]
    new = 0.95 * momentum_ref[0] + grad_ref[0].astype(jnp.float32)
    new_ref[0] = new
    moved_ref[...] = new.astype(jnp.bfloat16)


def momentum_step(source, grad, momentum, earlier):
    local_count, rows, columns = grad.shape
    step = row_block(rows, 128)
    spot = pl.BlockSpec((1, step, columns), lambda r, order: (order[0], r, 0))
    in_specs = [spot, spot]
    operands = [source, grad, momentum]
    aliases = {}
    if earlier is not None:
        in_specs.append(pl.BlockSpec(memory_space=pl.ANY))
        operands.append(earlier)
        aliases = {3: 0}
    return pl.pallas_call(
        momentum_kernel,
        grid_spec=pltpu.PrefetchScalarGridSpec(
            num_scalar_prefetch=1,
            grid=(rows // step,),
            in_specs=in_specs,
            out_specs=[spot, pl.BlockSpec((step, columns), lambda r, order: (r, 0))],
        ),
        out_shape=[
            jax.ShapeDtypeStruct(momentum.shape, jnp.float32),
            jax.ShapeDtypeStruct((rows, columns), jnp.bfloat16),
        ],
        input_output_aliases=aliases,
        compiler_params=pltpu.CompilerParams(vmem_limit_bytes=VMEM_BYTES),
        cost_estimate=SMALL_COST,
        name="momentum",
    )(*operands)


def block_places(columns):
    count = columns // BLOCK
    return [(i, j) for i in range(count) for j in range(i, count)]


def squares_tile(squares, index):
    top = float(jnp.finfo(jnp.bfloat16).max)
    spot = lax.broadcasted_iota(jnp.int32, (EXTRA_ROWS, BLOCK), 0) * BLOCK
    spot += lax.broadcasted_iota(jnp.int32, (EXTRA_ROWS, BLOCK), 1)
    tile = jnp.zeros((EXTRA_ROWS, BLOCK), jnp.float32)
    rest = squares
    for number in range(3):
        piece = jnp.minimum(rest, top).astype(jnp.bfloat16).astype(jnp.float32)
        tile = jnp.where(spot == 3 * index + number, piece, tile)
        rest = rest - piece
    return tile.astype(jnp.bfloat16)


def gram_kernel(where_ref, rows_ref, *refs):
    outputs, halves, sems = refs[:4], refs[4:6], refs[6]
    columns = rows_ref.shape[1]
    count = columns // BLOCK
    quarter = halves[0].shape[1] // BLOCK
    diagonal = lax.broadcasted_iota(jnp.int32, (BLOCK, BLOCK), 0) == lax.broadcasted_iota(
        jnp.int32, (BLOCK, BLOCK), 1
    )
    on_diagonal = jnp.zeros((BLOCK, BLOCK), jnp.float32)
    copies = []

    def send_out(half):
        upper = where_ref[half]
        for given in range(2):
            number = 2 * half + given
            source = upper if given == 0 else 1 - upper
            copy = pltpu.make_async_copy(
                halves[half].at[source], outputs[number], sems.at[number]
            )
            copy.start()
            copies.append(copy)

    place = 0
    for i in range(count):
        start = i * BLOCK
        strip = jnp.dot(
            rows_ref[:, start : start + BLOCK].T,
            rows_ref[:, start:],
            preferred_element_type=jnp.float32,
        )
        on_diagonal += jnp.where(diagonal, strip[:, :BLOCK], 0.0)
        for j in range(count - i):
            half, inside = divmod(place, 2 * quarter)
            part, slot = divmod(inside, quarter)
            halves[half][part, slot * BLOCK : (slot + 1) * BLOCK] = strip[
                :, j * BLOCK : (j + 1) * BLOCK
            ].astype(jnp.bfloat16)
            place += 1
            if place == 2 * quarter:
                send_out(0)
    squares = jnp.sum(on_diagonal, keepdims=True)
    halves[1][0, quarter * BLOCK :] = squares_tile(squares, where_ref[2])
    halves[1][1, quarter * BLOCK :] = jnp.zeros((EXTRA_ROWS, BLOCK), jnp.bfloat16)
    send_out(1)
    for copy in copies:
        copy.wait()


def gram_step(where, moved):
    columns = moved.shape[1]
    quarter = len(block_places(columns)) // 4 * BLOCK
    shapes = [(quarter, BLOCK), (quarter + EXTRA_ROWS, BLOCK)]
    return pl.pallas_call(
        gram_kernel,
        in_specs=[
            pl.BlockSpec(memory_space=pltpu.SMEM),
            pl.BlockSpec(memory_space=pltpu.VMEM),
        ],
        out_specs=[pl.BlockSpec(memory_space=pl.ANY)] * 4,
        out_shape=[jax.ShapeDtypeStruct(shapes[n // 2], jnp.bfloat16) for n in range(4)],
        scratch_shapes=[pltpu.VMEM((2, *shape), jnp.bfloat16) for shape in shapes]
        + [pltpu.SemaphoreType.DMA((4,))],
        compiler_params=pltpu.CompilerParams(vmem_limit_bytes=VMEM_BYTES),
        cost_estimate=SMALL_COST,
        name="gram",
    )(where, moved)


def times_gram(left_ref, gram_ref, j):
    start = j * BLOCK
    stop = start + BLOCK
    total = lax.dot_general(
        left_ref[:, start:],
        gram_ref[start:stop, start:],
        (((1,), (1,)), ((), ())),
        preferred_element_type=jnp.float32,
    )
    if j > 0:
        total += jnp.dot(
            left_ref[:, :start], gram_ref[:start, start:stop], preferred_element_type=jnp.float32
        )
    return total


def update_kernel(cuts, slot_ref, place_ref, rows_ref, *refs):
    pieces = refs[:4]
    gram_ref, normal_ref, product_ref = refs[-3:]
    out_refs = refs[-3 - cuts : -3]
    columns = gram_ref.shape[0]
    count = columns // BLOCK
    piece_blocks = pieces[0].shape[0] // BLOCK
    squares = sum(
        jnp.sum(piece[piece_blocks * BLOCK :].astype(jnp.float32), keepdims=True)
        for piece in pieces[2:]
    )
    factor = 0.5 * math.sqrt(columns) / jnp.sqrt(squares + 1e-06)
    factor_squared = factor * factor

    @pl.when(pl.program_id(0) == 0)
    def _():
        finite = squares < math.inf
        for number, piece in enumerate(pieces):
            for block in range(piece_blocks):
                index = number * piece_blocks + block
                row = pl.multiple_of(place_ref[0, index], BLOCK)
                column = pl.multiple_of(place_ref[1, index], BLOCK)
                value = piece[block * BLOCK : (block + 1) * BLOCK]
                gram_ref[pl.ds(row, BLOCK), pl.ds(column, BLOCK)] = jnp.where(
                    finite, value, jnp.zeros_like(value)
                )

    normal_ref[...] = (rows_ref[...].astype(jnp.float32) * factor).astype(jnp.bfloat16)
    for j in range(count):
        product = times_gram(normal_ref, gram_ref, j) * factor_squared
        product_ref[:, j * BLOCK : (j + 1) * BLOCK] = product.astype(jnp.bfloat16)
    for j in range(count):
        here = slice(j * BLOCK, (j + 1) * BLOCK)
        second = times_gram(product_ref, gram_ref, j) * factor_squared
        orthogonal = (
            3.4445 * normal_ref[:, here].astype(jnp.float32)
            - 4.775 * product_ref[:, here].astype(jnp.float32)
            + 2.0315 * second
        )
        result = (orthogonal * math.sqrt(D)).astype(jnp.bfloat16)
        for number, out_ref in enumerate(out_refs):

            @pl.when((pl.program_id(0) == number) | (cuts == 1))
            def _():
                out_ref[0, :, here] = result


def update_step(slot, places, moved, pieces, earlier=None, count=1):
    rows, columns = moved.shape
    step = rows // 2 if rows % 32 == 0 and rows >= 512 else rows
    in_specs = [pl.BlockSpec((step, columns), lambda r, *_: (r, 0))]
    in_specs += [pl.BlockSpec(piece.shape, lambda r, *_: (0, 0)) for piece in pieces]
    operands = [slot, places, moved, *pieces]
    if earlier is None:
        aliases = {}
        cuts = rows // step
        out_specs = [pl.BlockSpec((1, step, columns), lambda r, *_: (0, 0, 0))] * cuts
        out_shape = [jax.ShapeDtypeStruct((1, step, columns), jnp.bfloat16)] * cuts
    else:
        in_specs.append(pl.BlockSpec(memory_space=pl.ANY))
        operands.append(earlier)
        aliases = {7: 0}
        cuts = 1
        out_specs = [pl.BlockSpec((1, step, columns), lambda r, slot, *_: (slot[0], r, 0))]
        out_shape = [jax.ShapeDtypeStruct((count, rows, columns), jnp.bfloat16)]
    return pl.pallas_call(
        functools.partial(update_kernel, cuts),
        grid_spec=pltpu.PrefetchScalarGridSpec(
            num_scalar_prefetch=2,
            grid=(rows // step,),
            in_specs=in_specs,
            out_specs=out_specs,
            scratch_shapes=[
                pltpu.VMEM((columns, columns), jnp.bfloat16),
                pltpu.VMEM((step, columns), jnp.bfloat16),
                pltpu.VMEM((step, columns), jnp.bfloat16),
            ],
        ),
        out_shape=out_shape,
        input_output_aliases=aliases,
        compiler_params=pltpu.CompilerParams(vmem_limit_bytes=VMEM_BYTES),
        cost_estimate=SMALL_COST,
        name="update",
    )(*operands)


def place_kernel(cuts, slot_ref, *refs):
    for number in range(cuts):

        @pl.when(pl.program_id(0) == number)
        def _():
            refs[-1][...] = refs[number][...]


def place_step(slot, arrived, earlier, count):
    cuts = len(arrived)
    _, rows, columns = arrived[0].shape
    in_specs = [pl.BlockSpec((1, rows, columns), lambda r, slot: (0, 0, 0))] * cuts
    operands = [slot, *arrived]
    aliases = {}
    if earlier is not None:
        in_specs.append(pl.BlockSpec(memory_space=pl.ANY))
        operands.append(earlier)
        aliases = {cuts + 1: 0}
    return pl.pallas_call(
        functools.partial(place_kernel, cuts),
        grid_spec=pltpu.PrefetchScalarGridSpec(
            num_scalar_prefetch=1,
            grid=(cuts,),
            in_specs=in_specs,
            out_specs=pl.BlockSpec((1, rows, columns), lambda r, slot: (slot[0], r, 0)),
        ),
        out_shape=jax.ShapeDtypeStruct((count, cuts * rows, columns), jnp.bfloat16),
        input_output_aliases=aliases,
        compiler_params=pltpu.CompilerParams(vmem_limit_bytes=VMEM_BYTES),
        cost_estimate=SMALL_COST,
        name="place",
    )(*operands)


def add_up(mine, arrived):
    return (mine.astype(jnp.float32) + arrived.astype(jnp.float32)).astype(jnp.bfloat16)


class Routes:
    def __init__(self, dp_count):
        everyone = range(dp_count)
        line = lambda i: i >> 1 & 3
        self.side = [(i, i ^ 1) for i in everyone]
        self.inner_side = [(i, i ^ 1) for i in everyone if line(i) in (1, 2)]
        self.inward = [(i, i + 2) for i in everyone if line(i) == 0]
        self.inward += [(i, i - 2) for i in everyone if line(i) == 3]
        self.outward = [(b, a) for a, b in self.inward]
        self.middle = [(i, i + 2) for i in everyone if line(i) == 1]
        self.middle += [(i, i - 2) for i in everyone if line(i) == 2]
        self.far = []
        distance = 8
        while distance < dp_count:
            self.far.append([(i, i ^ distance) for i in everyone])
            distance *= 2


def send(value, pairs):
    return lax.ppermute(value, "dp", pairs)


class SideFirst:
    hops = {
        "side": ("side", (), 0),
        "in": ("inward", ("side",), 1),
        "middle": ("middle", ("in",), 1),
        "out": ("outward", ("middle",), 1),
        "gather": ("side", ("out",), 1),
    }

    def __init__(self, routes, place, kept, given):
        self.routes, self.inner = routes, place.inner
        self.kept, self.given = kept, given

    def value(self, hop, got):
        if hop == "side":
            return self.given
        if hop == "in":
            self.total = add_up(self.kept, got["side"])
        elif hop == "middle":
            self.total = add_up(self.total, got["in"])
        elif hop == "out":
            self.total = add_up(self.total, got["middle"])
            for pairs in self.routes.far:
                self.total = add_up(self.total, send(self.total, pairs))
        else:
            self.total = jnp.where(self.inner, self.total, got["out"])
        return self.total

    def pieces(self, got):
        return self.total, got["gather"]


class LineFirst:
    hops = {
        "in given": ("inward", (), 0),
        "in kept": ("inward", (), 0),
        "middle": ("middle", ("in given",), 1),
        "side": ("inner_side", ("in kept", "middle"), 2),
        "middle back": ("middle", ("side",), 1),
        "out": ("outward", ("side",), 0),
        "out other": ("outward", ("middle back",), 0),
    }

    def __init__(self, routes, place, kept, given):
        self.routes, self.inner = routes, place.inner
        self.kept, self.given = kept, given
        self.total = None

    def value(self, hop, got):
        if hop == "in given":
            return self.given
        if hop == "in kept":
            return self.kept
        if hop == "middle":
            return add_up(self.given, got["in given"])
        if hop == "side":
            self.kept = add_up(add_up(self.kept, got["in kept"]), got["middle"])
            return self.kept
        if hop == "out other":
            return got["middle back"]
        if self.total is None:
            self.total = add_up(self.kept, got["side"])
            for pairs in self.routes.far:
                self.total = add_up(self.total, send(self.total, pairs))
        return self.total

    def pieces(self, got):
        return (
            jnp.where(self.inner, self.total, got["out"]),
            jnp.where(self.inner, got["middle back"], got["out other"]),
        )


def plan(experts):
    transfer, latency, issue, pass_over = 23.3, 3.0, 2.5, 1.8
    takes = {"momentum": 12.0, "gram": 9.0, "update": 28.0, "place": 5.0}
    near, far = 12.0, 96.0
    deepest, patience, backlog = 4, 4.0, 10.0
    hops = {}
    for expert in range(experts):
        for kind in (LineFirst, SideFirst):
            for name, (link, needs, passes) in kind.hops.items():
                needed = [(expert, kind, need) for need in needs]
                hops[expert, kind, name] = (link.replace("inner_", ""), needed, passes)
    lengths = {}

    def length(hop):
        if hop not in lengths:
            later = [length(h) for h in hops if hop in hops[h][1]]
            lengths[hop] = 1 + max(later, default=0)
        return lengths[hop]

    def rank(hop):
        return hop[0] - length(hop) - (0.5 if hop[1] is SideFirst else 0), hop[0]

    first_choice = sorted(hops, key=rank)
    order = []
    now = 0.0
    count = dict.fromkeys(takes, 0)
    arrival = {}
    queues = {link: [] for link, _, _ in hops.values()}
    update_arrival = {}
    far_free = 0.0
    halfway = {}
    taken = set()

    def put(action, which):
        arrived = [hop for hop in arrival if arrival[hop] <= now and hop not in taken]
        taken.update(arrived)
        order.append((action, which, arrived))

    def do(kernel):
        nonlocal now
        put(kernel, count[kernel])
        count[kernel] += 1
        now += takes[kernel]

    def next_hop():
        for hop in first_choice:
            link, needed, _ = hops[hop]
            queued = sum(time > now for time in queues[link])
            if hop[0] < count["gram"] and hop not in arrival and queued < deepest:
                if all(arrival.get(need, math.inf) <= now for need in needed):
                    return hop
        return None

    do("momentum")
    do("gram")
    while count["place"] < experts - 1:
        updating = count["update"]
        last = updating == experts - 1
        mine = [h for h in hops if h[0] == updating]
        whole = updating < experts and all(arrival.get(h, math.inf) <= now for h in mine)
        if updating == experts - 2:
            whole = whole and len(arrival) == len(hops)
        if last:
            whole = whole and update_arrival.get(count["place"], math.inf) > now
        coming = min((time for time in arrival.values() if time > now), default=math.inf)
        ahead = min(max([0.0] + [time - now for time in queue]) for queue in queues.values())
        free = last or coming - now >= patience or ahead >= backlog
        hop = next_hop()
        if hop is not None:
            link, _, passes = hops[hop]
            put("hop", hop)
            now += issue + passes * pass_over
            queue = queues[link]
            queue.append(max([now + 1, *queue[-1:]]) + transfer)
            arrival[hop] = queue[-1] + latency
        elif count["gram"] < count["momentum"]:
            do("gram")
        elif count["momentum"] < experts:
            do("momentum")
        elif whole and free:
            do("update")
            if updating < experts - 2:
                halfway[updating] = max(now, far_free) + far / 3
                far_free = max(now, far_free) + far
                update_arrival[updating] = far_free
            else:
                update_arrival[updating] = now + near
        elif any(time <= now for time in halfway.values()):
            put("half", min(halfway))
            del halfway[min(halfway)]
        elif update_arrival.get(count["place"], math.inf) <= now:
            do("place")
        else:
            times = [*arrival.values(), *update_arrival.values(), *halfway.values()]
            now = min(time for time in times if time > now)
    return order


class Place:
    def __init__(self, index):
        line = index >> 1 & 3
        self.side = index & 1
        self.upper_line = line >> 1
        self.inner = (line == 1) | (line == 2)


def shards(grad, momentum, placement):
    local_count, row_count, columns = grad.shape
    group_count = lax.axis_size("expert")
    routes = Routes(lax.axis_size("dp"))
    my_group = lax.axis_index("expert")
    my_place = Place(lax.axis_index("dp"))

    slot_ids = lax.iota(jnp.int32, local_count)
    moves = placement.reshape(group_count, local_count)

    def route(group, target):
        row = lax.dynamic_index_in_dim(moves, group, keepdims=False)
        chosen = row // local_count == target
        old_slot = jnp.sum(jnp.where(chosen, slot_ids, 0))
        new_slot = jnp.sum(jnp.where(chosen, row % local_count, 0))
        return old_slot, new_slot

    places = jnp.array(block_places(columns), jnp.int32) * BLOCK
    quarter = places.shape[0] // 4
    quarters = places.reshape(4, quarter, 2)
    order = jnp.stack(
        [my_place.side, 1 - my_place.side, 2 + my_place.upper_line, 3 - my_place.upper_line]
    )
    my_places = jnp.take(quarters, order, axis=0).reshape(4 * quarter, 2).T

    where = jnp.stack([my_place.side, my_place.upper_line, lax.axis_index("dp")])

    distances = list(range(group_count - 1, -1, -1))
    momentum_new = None
    update = None
    moved, chains, got, leaving = {}, {}, {}, {}
    front = ()

    def follow(*values):
        return lax.optimization_barrier((values, front))[0]

    for action, which, arrived_hops in plan(group_count):
        taken = follow(*[got[e, kind][name] for e, kind, name in arrived_hops])
        for (e, kind, name), arrival in zip(arrived_hops, taken):
            got[e, kind][name] = arrival
        front = (*front, *taken)
        if action == "hop":
            e, kind, name = which
            needs = kind.hops[name][1]
            arrived = dict(zip(needs, follow(*[got[e, kind][need] for need in needs])))
            (value,) = follow(chains[e, kind].value(name, arrived))
            got[e, kind][name] = send(value, getattr(routes, kind.hops[name][0]))
            front = (value,)
        elif action == "momentum":
            old_slot, _ = route(my_group, my_group ^ distances[which])
            (old_slot,) = follow(old_slot.reshape(1))
            momentum_new, moved[which] = momentum_step(old_slot, grad, momentum, momentum_new)
            front = (moved[which],)
        elif action == "gram":
            (rows,) = follow(moved[which])
            parts = gram_step(where, rows)
            chains[which, SideFirst] = SideFirst(routes, my_place, *parts[:2])
            chains[which, LineFirst] = LineFirst(routes, my_place, *parts[2:])
            got[which, SideFirst], got[which, LineFirst] = {}, {}
            front = tuple(parts[3:])
        elif action == "update":
            pieces = chains[which, SideFirst].pieces(got[which, SideFirst])
            pieces += chains[which, LineFirst].pieces(got[which, LineFirst])
            pieces = follow(*pieces)
            new_slot = route(my_group ^ distances[which], my_group)[1].reshape(1)
            rows = moved[which]
            if distances[which] == 0:
                (update,) = update_step(
                    new_slot, my_places, rows, pieces, update, local_count
                )
                front = (update,)
            else:
                here = jnp.zeros((1,), jnp.int32)
                cuts = update_step(here, my_places, rows, pieces)
                front = (cuts[0],)
                if distances[which] == 1 and row_count % 64 == 0:
                    cuts = [part for cut in cuts for part in jnp.split(cut, 4 // len(cuts), axis=1)]
                pairs = [(g, g ^ distances[which]) for g in range(group_count)]
                leaving[which] = new_slot, [lax.ppermute(cut, "expert", pairs) for cut in cuts]
        elif action == "half":
            new_slot, arrived = leaving[which]
            front = (*front, *follow(arrived[0]))
            leaving[which] = new_slot, [front[-1], *arrived[1:]]
        else:
            new_slot, arrived = leaving[which]
            (new_slot,) = follow(new_slot)
            update = place_step(new_slot, arrived, update, local_count)
            front = (update,)
    return momentum_new, update


def solution(mesh):
    return jax.shard_map(
        shards,
        mesh=mesh,
        in_specs=(P("expert", "dp", None), P("expert", "dp", None), P()),
        out_specs=(P("expert", "dp", None), P("expert", "dp", None)),
        check_vma=False,
    )
```

```python
import functools
import math

import jax
import jax.numpy as jnp
from jax import lax
from jax.experimental import pallas as pl
from jax.experimental.pallas import tpu as pltpu
from jax.sharding import PartitionSpec as P

D = 7168
BLOCK = 256
EXTRA_ROWS = 16
VMEM_BYTES = 56 * 2**20
SMALL_COST = pl.CostEstimate(flops=2**20, bytes_accessed=2**10, transcendentals=0)


def row_block(rows, most):
    for size in range(most, 15, -16):
        if rows % size == 0:
            return size
    return rows


def momentum_kernel(order_ref, grad_ref, momentum_ref, *refs):
    new_ref, moved_ref = refs[-2:]
    new = 0.95 * momentum_ref[0] + grad_ref[0].astype(jnp.float32)
    new_ref[0] = new
    moved_ref[...] = new.astype(jnp.bfloat16)


def momentum_step(source, grad, momentum, earlier):
    local_count, rows, columns = grad.shape
    step = row_block(rows, 128)
    spot = pl.BlockSpec((1, step, columns), lambda r, order: (order[0], r, 0))
    in_specs = [spot, spot]
    operands = [source, grad, momentum]
    aliases = {}
    if earlier is not None:
        in_specs.append(pl.BlockSpec(memory_space=pl.ANY))
        operands.append(earlier)
        aliases = {3: 0}
    return pl.pallas_call(
        momentum_kernel,
        grid_spec=pltpu.PrefetchScalarGridSpec(
            num_scalar_prefetch=1,
            grid=(rows // step,),
            in_specs=in_specs,
            out_specs=[spot, pl.BlockSpec((step, columns), lambda r, order: (r, 0))],
        ),
        out_shape=[
            jax.ShapeDtypeStruct(momentum.shape, jnp.float32),
            jax.ShapeDtypeStruct((rows, columns), jnp.bfloat16),
        ],
        input_output_aliases=aliases,
        compiler_params=pltpu.CompilerParams(vmem_limit_bytes=VMEM_BYTES),
        cost_estimate=SMALL_COST,
        name="momentum",
    )(*operands)


def block_places(columns):
    count = columns // BLOCK
    return [(i, j) for j in range(count) for i in range(j + 1)]


def squares_tile(squares, index):
    top = float(jnp.finfo(jnp.bfloat16).max)
    spot = lax.broadcasted_iota(jnp.int32, (EXTRA_ROWS, BLOCK), 0) * BLOCK
    spot += lax.broadcasted_iota(jnp.int32, (EXTRA_ROWS, BLOCK), 1)
    tile = jnp.zeros((EXTRA_ROWS, BLOCK), jnp.float32)
    rest = squares
    for number in range(3):
        piece = jnp.minimum(rest, top).astype(jnp.bfloat16).astype(jnp.float32)
        tile = jnp.where(spot == 3 * index + number, piece, tile)
        rest = rest - piece
    return tile.astype(jnp.bfloat16)


def gram_kernel(where_ref, rows_ref, *refs):
    outputs, halves, sems, turned_ref = refs[:4], refs[4:6], refs[6], refs[7]
    columns = rows_ref.shape[1]
    count = columns // BLOCK
    quarter = halves[0].shape[1] // BLOCK
    diagonal = lax.broadcasted_iota(jnp.int32, (BLOCK, BLOCK), 0) == lax.broadcasted_iota(
        jnp.int32, (BLOCK, BLOCK), 1
    )
    on_diagonal = jnp.zeros((BLOCK, BLOCK), jnp.float32)
    copies = []

    def send_out(half):
        upper = where_ref[half]
        for given in range(2):
            number = 2 * half + given
            source = upper if given == 0 else 1 - upper
            copy = pltpu.make_async_copy(
                halves[half].at[source], outputs[number], sems.at[number]
            )
            copy.start()
            copies.append(copy)

    place = 0
    for j in range(count):
        start = j * BLOCK
        stop = start + BLOCK
        turned_ref[start:stop] = rows_ref[:, start:stop].T
        strip = jnp.dot(
            turned_ref[:stop], rows_ref[:, start:stop], preferred_element_type=jnp.float32
        )
        on_diagonal += jnp.where(diagonal, strip[start:], 0.0)
        for i in range(j + 1):
            half, inside = divmod(place, 2 * quarter)
            part, slot = divmod(inside, quarter)
            halves[half][part, slot * BLOCK : (slot + 1) * BLOCK] = strip[
                i * BLOCK : (i + 1) * BLOCK
            ].astype(jnp.bfloat16)
            place += 1
            if place == 2 * quarter:
                send_out(0)
    squares = jnp.sum(on_diagonal, keepdims=True)
    halves[1][0, quarter * BLOCK :] = squares_tile(squares, where_ref[2])
    halves[1][1, quarter * BLOCK :] = jnp.zeros((EXTRA_ROWS, BLOCK), jnp.bfloat16)
    send_out(1)
    for copy in copies:
        copy.wait()


def gram_step(where, moved):
    columns = moved.shape[1]
    quarter = len(block_places(columns)) // 4 * BLOCK
    shapes = [(quarter, BLOCK), (quarter + EXTRA_ROWS, BLOCK)]
    return pl.pallas_call(
        gram_kernel,
        in_specs=[
            pl.BlockSpec(memory_space=pltpu.SMEM),
            pl.BlockSpec(memory_space=pltpu.VMEM),
        ],
        out_specs=[pl.BlockSpec(memory_space=pl.ANY)] * 4,
        out_shape=[jax.ShapeDtypeStruct(shapes[n // 2], jnp.bfloat16) for n in range(4)],
        scratch_shapes=[pltpu.VMEM((2, *shape), jnp.bfloat16) for shape in shapes]
        + [pltpu.SemaphoreType.DMA((4,)), pltpu.VMEM(moved.shape[::-1], jnp.bfloat16)],
        compiler_params=pltpu.CompilerParams(vmem_limit_bytes=VMEM_BYTES),
        cost_estimate=SMALL_COST,
        name="gram",
    )(where, moved)


def times_gram(left_ref, gram_ref, j):
    start = j * BLOCK
    stop = start + BLOCK
    total = lax.dot_general(
        left_ref[:, start:],
        gram_ref[start:stop, start:],
        (((1,), (1,)), ((), ())),
        preferred_element_type=jnp.float32,
    )
    if j > 0:
        total += jnp.dot(
            left_ref[:, :start], gram_ref[:start, start:stop], preferred_element_type=jnp.float32
        )
    return total


def update_kernel(slot_ref, place_ref, rows_ref, *refs):
    pieces = refs[:4]
    out_ref, gram_ref, normal_ref, product_ref = refs[-4:]
    columns = gram_ref.shape[0]
    count = columns // BLOCK
    piece_blocks = pieces[0].shape[0] // BLOCK
    squares = sum(
        jnp.sum(piece[piece_blocks * BLOCK :].astype(jnp.float32), keepdims=True)
        for piece in pieces[2:]
    )
    factor = 0.5 * math.sqrt(columns) / jnp.sqrt(squares + 1e-06)
    factor_squared = factor * factor

    @pl.when(pl.program_id(0) == 0)
    def _():
        finite = squares < math.inf
        for number, piece in enumerate(pieces):
            for block in range(piece_blocks):
                index = number * piece_blocks + block
                row = pl.multiple_of(place_ref[0, index], BLOCK)
                column = pl.multiple_of(place_ref[1, index], BLOCK)
                value = piece[block * BLOCK : (block + 1) * BLOCK]
                gram_ref[pl.ds(row, BLOCK), pl.ds(column, BLOCK)] = jnp.where(
                    finite, value, jnp.zeros_like(value)
                )

    normal_ref[...] = (rows_ref[...].astype(jnp.float32) * factor).astype(jnp.bfloat16)
    for j in range(count):
        product = times_gram(normal_ref, gram_ref, j) * factor_squared
        product_ref[:, j * BLOCK : (j + 1) * BLOCK] = product.astype(jnp.bfloat16)
    for j in range(count):
        here = slice(j * BLOCK, (j + 1) * BLOCK)
        second = times_gram(product_ref, gram_ref, j) * factor_squared
        orthogonal = (
            3.4445 * normal_ref[:, here].astype(jnp.float32)
            - 4.775 * product_ref[:, here].astype(jnp.float32)
            + 2.0315 * second
        )
        out_ref[0, :, here] = (orthogonal * math.sqrt(D)).astype(jnp.bfloat16)


def update_step(slot, places, moved, pieces, earlier=None, count=1):
    rows, columns = moved.shape
    step = rows
    in_specs = [pl.BlockSpec((step, columns), lambda r, *_: (r, 0))]
    in_specs += [pl.BlockSpec(piece.shape, lambda r, *_: (0, 0)) for piece in pieces]
    operands = [slot, places, moved, *pieces]
    aliases = {}
    if earlier is not None:
        in_specs.append(pl.BlockSpec(memory_space=pl.ANY))
        operands.append(earlier)
        aliases = {7: 0}
    return pl.pallas_call(
        update_kernel,
        grid_spec=pltpu.PrefetchScalarGridSpec(
            num_scalar_prefetch=2,
            grid=(rows // step,),
            in_specs=in_specs,
            out_specs=pl.BlockSpec((1, step, columns), lambda r, slot, *_: (slot[0], r, 0)),
            scratch_shapes=[
                pltpu.VMEM((columns, columns), jnp.bfloat16),
                pltpu.VMEM((step, columns), jnp.bfloat16),
                pltpu.VMEM((step, columns), jnp.bfloat16),
            ],
        ),
        out_shape=jax.ShapeDtypeStruct((count, rows, columns), jnp.bfloat16),
        input_output_aliases=aliases,
        compiler_params=pltpu.CompilerParams(vmem_limit_bytes=VMEM_BYTES),
        cost_estimate=SMALL_COST,
        name="update",
    )(*operands)


def place_kernel(cuts, slot_ref, *refs):
    for number in range(cuts):

        @pl.when(pl.program_id(0) == number)
        def _():
            refs[-1][...] = refs[number][...]


def place_step(slot, arrived, earlier, count):
    cuts = len(arrived)
    _, rows, columns = arrived[0].shape
    in_specs = [pl.BlockSpec((1, rows, columns), lambda r, slot: (0, 0, 0))] * cuts
    operands = [slot, *arrived]
    aliases = {}
    if earlier is not None:
        in_specs.append(pl.BlockSpec(memory_space=pl.ANY))
        operands.append(earlier)
        aliases = {cuts + 1: 0}
    return pl.pallas_call(
        functools.partial(place_kernel, cuts),
        grid_spec=pltpu.PrefetchScalarGridSpec(
            num_scalar_prefetch=1,
            grid=(cuts,),
            in_specs=in_specs,
            out_specs=pl.BlockSpec((1, rows, columns), lambda r, slot: (slot[0], r, 0)),
        ),
        out_shape=jax.ShapeDtypeStruct((count, cuts * rows, columns), jnp.bfloat16),
        input_output_aliases=aliases,
        compiler_params=pltpu.CompilerParams(vmem_limit_bytes=VMEM_BYTES),
        cost_estimate=SMALL_COST,
        name="place",
    )(*operands)


def add_up(mine, arrived):
    return (mine.astype(jnp.float32) + arrived.astype(jnp.float32)).astype(jnp.bfloat16)


class Routes:
    def __init__(self, dp_count):
        everyone = range(dp_count)
        line = lambda i: i >> 1 & 3
        self.side = [(i, i ^ 1) for i in everyone]
        self.inner_side = [(i, i ^ 1) for i in everyone if line(i) in (1, 2)]
        self.inward = [(i, i + 2) for i in everyone if line(i) == 0]
        self.inward += [(i, i - 2) for i in everyone if line(i) == 3]
        self.outward = [(b, a) for a, b in self.inward]
        self.middle = [(i, i + 2) for i in everyone if line(i) == 1]
        self.middle += [(i, i - 2) for i in everyone if line(i) == 2]
        self.far = []
        distance = 8
        while distance < dp_count:
            self.far.append([(i, i ^ distance) for i in everyone])
            distance *= 2


def send(value, pairs):
    return lax.ppermute(value, "dp", pairs)


class SideFirst:
    hops = {
        "side": ("side", (), 0),
        "in": ("inward", ("side",), 1),
        "middle": ("middle", ("in",), 1),
        "out": ("outward", ("middle",), 1),
        "gather": ("side", ("out",), 1),
    }

    def __init__(self, routes, place, kept, given):
        self.routes, self.inner = routes, place.inner
        self.kept, self.given = kept, given

    def value(self, hop, got):
        if hop == "side":
            return self.given
        if hop == "in":
            self.total = add_up(self.kept, got["side"])
        elif hop == "middle":
            self.total = add_up(self.total, got["in"])
        elif hop == "out":
            self.total = add_up(self.total, got["middle"])
            for pairs in self.routes.far:
                self.total = add_up(self.total, send(self.total, pairs))
        else:
            self.total = jnp.where(self.inner, self.total, got["out"])
        return self.total

    def pieces(self, got):
        return self.total, got["gather"]


class LineFirst:
    hops = {
        "in given": ("inward", (), 0),
        "in kept": ("inward", (), 0),
        "middle": ("middle", ("in given",), 1),
        "side": ("inner_side", ("in kept", "middle"), 2),
        "middle back": ("middle", ("side",), 1),
        "out": ("outward", ("side",), 0),
        "out other": ("outward", ("middle back",), 0),
    }

    def __init__(self, routes, place, kept, given):
        self.routes, self.inner = routes, place.inner
        self.kept, self.given = kept, given
        self.total = None

    def value(self, hop, got):
        if hop == "in given":
            return self.given
        if hop == "in kept":
            return self.kept
        if hop == "middle":
            return add_up(self.given, got["in given"])
        if hop == "side":
            self.kept = add_up(add_up(self.kept, got["in kept"]), got["middle"])
            return self.kept
        if hop == "out other":
            return got["middle back"]
        if self.total is None:
            self.total = add_up(self.kept, got["side"])
            for pairs in self.routes.far:
                self.total = add_up(self.total, send(self.total, pairs))
        return self.total

    def pieces(self, got):
        return (
            jnp.where(self.inner, self.total, got["out"]),
            jnp.where(self.inner, got["middle back"], got["out other"]),
        )


def plan(experts):
    transfer, latency, issue, pass_over = 23.3, 3.0, 2.5, 1.8
    takes = {"momentum": 12.0, "gram": 9.0, "update": 28.0, "place": 5.0}
    near, far = 12.0, 78.0
    deepest, patience, backlog = 4, 4.0, 10.0
    hops = {}
    for expert in range(experts):
        for kind in (LineFirst, SideFirst):
            for name, (link, needs, passes) in kind.hops.items():
                needed = [(expert, kind, need) for need in needs]
                hops[expert, kind, name] = (link.replace("inner_", ""), needed, passes)
    lengths = {}

    def length(hop):
        if hop not in lengths:
            later = [length(h) for h in hops if hop in hops[h][1]]
            lengths[hop] = 1 + max(later, default=0)
        return lengths[hop]

    def rank(hop):
        return hop[0] - length(hop) - (0.5 if hop[1] is SideFirst else 0), hop[0]

    first_choice = sorted(hops, key=rank)
    order = []
    now = 0.0
    count = dict.fromkeys(takes, 0)
    arrival = {}
    queues = {link: [] for link, _, _ in hops.values()}
    update_arrival = {}
    far_free = 0.0
    taken = set()

    def put(action, which):
        arrived = [hop for hop in arrival if arrival[hop] <= now and hop not in taken]
        taken.update(arrived)
        order.append((action, which, arrived))

    def do(kernel):
        nonlocal now
        put(kernel, count[kernel])
        count[kernel] += 1
        now += takes[kernel]

    def next_hop():
        for hop in first_choice:
            link, needed, _ = hops[hop]
            queued = sum(time > now for time in queues[link])
            if hop[0] < count["gram"] and hop not in arrival and queued < deepest:
                if all(arrival.get(need, math.inf) <= now for need in needed):
                    return hop
        return None

    do("momentum")
    do("gram")
    while count["place"] < experts - 1:
        updating = count["update"]
        last = updating == experts - 1
        early = count["place"] < experts - 3 or updating == experts
        mine = [h for h in hops if h[0] == updating]
        whole = updating < experts and all(arrival.get(h, math.inf) <= now for h in mine)
        if updating == experts - 2:
            whole = whole and len(arrival) == len(hops)
        if last:
            whole = whole and count["place"] >= experts - 3
        coming = min((time for time in arrival.values() if time > now), default=math.inf)
        ahead = min(max([0.0] + [time - now for time in queue]) for queue in queues.values())
        free = last or coming - now >= patience or ahead >= backlog
        hop = next_hop()
        if hop is not None:
            link, _, passes = hops[hop]
            put("hop", hop)
            now += issue + passes * pass_over
            queue = queues[link]
            queue.append(max([now + 1, *queue[-1:]]) + transfer)
            arrival[hop] = queue[-1] + latency
        elif count["gram"] < count["momentum"]:
            do("gram")
        elif count["momentum"] < experts:
            do("momentum")
        elif whole and free:
            do("update")
            if updating < experts - 2:
                far_free = max(now, far_free) + far
                update_arrival[updating] = far_free
            else:
                update_arrival[updating] = now + near
        elif early and update_arrival.get(count["place"], math.inf) <= now:
            do("place")
        else:
            times = [*arrival.values(), *update_arrival.values()]
            now = min(time for time in times if time > now)
    return order


class Place:
    def __init__(self, index):
        line = index >> 1 & 3
        self.side = index & 1
        self.upper_line = line >> 1
        self.inner = (line == 1) | (line == 2)


def shards(grad, momentum, placement):
    local_count, row_count, columns = grad.shape
    group_count = lax.axis_size("expert")
    routes = Routes(lax.axis_size("dp"))
    my_group = lax.axis_index("expert")
    my_place = Place(lax.axis_index("dp"))

    slot_ids = lax.iota(jnp.int32, local_count)
    moves = placement.reshape(group_count, local_count)

    def route(group, target):
        row = lax.dynamic_index_in_dim(moves, group, keepdims=False)
        chosen = row // local_count == target
        old_slot = jnp.sum(jnp.where(chosen, slot_ids, 0))
        new_slot = jnp.sum(jnp.where(chosen, row % local_count, 0))
        return old_slot, new_slot

    places = jnp.array(block_places(columns), jnp.int32) * BLOCK
    quarter = places.shape[0] // 4
    quarters = places.reshape(4, quarter, 2)
    order = jnp.stack(
        [my_place.side, 1 - my_place.side, 2 + my_place.upper_line, 3 - my_place.upper_line]
    )
    my_places = jnp.take(quarters, order, axis=0).reshape(4 * quarter, 2).T

    where = jnp.stack([my_place.side, my_place.upper_line, lax.axis_index("dp")])

    distances = list(range(group_count - 1, -1, -1))
    momentum_new = None
    update = None
    moved, chains, got, leaving = {}, {}, {}, {}
    front = ()

    def follow(*values):
        return lax.optimization_barrier((values, front))[0]

    for action, which, arrived_hops in plan(group_count):
        taken = follow(*[got[e, kind][name] for e, kind, name in arrived_hops])
        for (e, kind, name), arrival in zip(arrived_hops, taken):
            got[e, kind][name] = arrival
        front = (*front, *taken)
        if action == "hop":
            e, kind, name = which
            needs = kind.hops[name][1]
            arrived = dict(zip(needs, follow(*[got[e, kind][need] for need in needs])))
            (value,) = follow(chains[e, kind].value(name, arrived))
            got[e, kind][name] = send(value, getattr(routes, kind.hops[name][0]))
            front = (value,)
        elif action == "momentum":
            old_slot, _ = route(my_group, my_group ^ distances[which])
            (old_slot,) = follow(old_slot.reshape(1))
            momentum_new, moved[which] = momentum_step(old_slot, grad, momentum, momentum_new)
            front = (moved[which],)
        elif action == "gram":
            (rows,) = follow(moved[which])
            parts = gram_step(where, rows)
            chains[which, SideFirst] = SideFirst(routes, my_place, *parts[:2])
            chains[which, LineFirst] = LineFirst(routes, my_place, *parts[2:])
            got[which, SideFirst], got[which, LineFirst] = {}, {}
            front = tuple(parts[3:])
        elif action == "update":
            pieces = chains[which, SideFirst].pieces(got[which, SideFirst])
            pieces += chains[which, LineFirst].pieces(got[which, LineFirst])
            pieces = follow(*pieces)
            new_slot = route(my_group ^ distances[which], my_group)[1].reshape(1)
            rows = moved[which]
            if distances[which] == 0:
                update = update_step(
                    new_slot, my_places, rows, pieces, update, local_count
                )
                front = (update,)
            else:
                here = jnp.zeros((1,), jnp.int32)
                mine = update_step(here, my_places, rows, pieces)
                pairs = [(g, g ^ distances[which]) for g in range(group_count)]
                cuts = 4 if distances[which] == 1 and row_count % 64 == 0 else 1
                cut_rows = [
                    lax.ppermute(cut, "expert", pairs) for cut in jnp.split(mine, cuts, axis=1)
                ]
                leaving[which] = new_slot, cut_rows
                front = (mine,)
        else:
            new_slot, arrived = leaving[which]
            (new_slot,) = follow(new_slot)
            update = place_step(new_slot, arrived, update, local_count)
            front = (update,)
    return momentum_new, update


def solution(mesh):
    return jax.shard_map(
        shards,
        mesh=mesh,
        in_specs=(P("expert", "dp", None), P("expert", "dp", None), P()),
        out_specs=(P("expert", "dp", None), P("expert", "dp", None)),
        check_vma=False,
    )
```

```python
import functools
import math

import jax
import jax.numpy as jnp
from jax import lax
from jax.experimental import pallas as pl
from jax.experimental.pallas import tpu as pltpu
from jax.sharding import PartitionSpec as P

D = 7168
BLOCK = 256
EXTRA_ROWS = 16
VMEM_BYTES = 56 * 2**20
SMALL_COST = pl.CostEstimate(flops=2**20, bytes_accessed=2**10, transcendentals=0)


def row_block(rows, most):
    for size in range(most, 15, -16):
        if rows % size == 0:
            return size
    return rows


def momentum_kernel(order_ref, grad_ref, momentum_ref, *refs):
    new_ref, moved_ref = refs[-2:]
    new = 0.95 * momentum_ref[0] + grad_ref[0].astype(jnp.float32)
    new_ref[0] = new
    moved_ref[...] = new.astype(jnp.bfloat16)


def momentum_step(source, grad, momentum, earlier):
    local_count, rows, columns = grad.shape
    step = row_block(rows, 128)
    spot = pl.BlockSpec((1, step, columns), lambda r, order: (order[0], r, 0))
    in_specs = [spot, spot]
    operands = [source, grad, momentum]
    aliases = {}
    if earlier is not None:
        in_specs.append(pl.BlockSpec(memory_space=pl.ANY))
        operands.append(earlier)
        aliases = {3: 0}
    return pl.pallas_call(
        momentum_kernel,
        grid_spec=pltpu.PrefetchScalarGridSpec(
            num_scalar_prefetch=1,
            grid=(rows // step,),
            in_specs=in_specs,
            out_specs=[spot, pl.BlockSpec((step, columns), lambda r, order: (r, 0))],
        ),
        out_shape=[
            jax.ShapeDtypeStruct(momentum.shape, jnp.float32),
            jax.ShapeDtypeStruct((rows, columns), jnp.bfloat16),
        ],
        input_output_aliases=aliases,
        compiler_params=pltpu.CompilerParams(vmem_limit_bytes=VMEM_BYTES),
        cost_estimate=SMALL_COST,
        name="momentum",
    )(*operands)


def block_places(columns):
    count = columns // BLOCK
    return [(i, j) for j in range(count) for i in range(j + 1)]


def squares_tile(squares, index):
    top = float(jnp.finfo(jnp.bfloat16).max)
    spot = lax.broadcasted_iota(jnp.int32, (EXTRA_ROWS, BLOCK), 0) * BLOCK
    spot += lax.broadcasted_iota(jnp.int32, (EXTRA_ROWS, BLOCK), 1)
    tile = jnp.zeros((EXTRA_ROWS, BLOCK), jnp.float32)
    rest = squares
    for number in range(3):
        piece = jnp.minimum(rest, top).astype(jnp.bfloat16).astype(jnp.float32)
        tile = jnp.where(spot == 3 * index + number, piece, tile)
        rest = rest - piece
    return tile.astype(jnp.bfloat16)


def gram_kernel(where_ref, rows_ref, *refs):
    outputs, halves, sems, turned_ref = refs[:4], refs[4:6], refs[6], refs[7]
    columns = rows_ref.shape[1]
    count = columns // BLOCK
    quarter = halves[0].shape[1] // BLOCK
    diagonal = lax.broadcasted_iota(jnp.int32, (BLOCK, BLOCK), 0) == lax.broadcasted_iota(
        jnp.int32, (BLOCK, BLOCK), 1
    )
    on_diagonal = jnp.zeros((BLOCK, BLOCK), jnp.float32)
    copies = []

    def send_out(half):
        upper = where_ref[half]
        for given in range(2):
            number = 2 * half + given
            source = upper if given == 0 else 1 - upper
            copy = pltpu.make_async_copy(
                halves[half].at[source], outputs[number], sems.at[number]
            )
            copy.start()
            copies.append(copy)

    place = 0
    for j in range(count):
        start = j * BLOCK
        stop = start + BLOCK
        turned_ref[start:stop] = rows_ref[:, start:stop].T
        strip = jnp.dot(
            turned_ref[:stop], rows_ref[:, start:stop], preferred_element_type=jnp.float32
        )
        on_diagonal += jnp.where(diagonal, strip[start:], 0.0)
        for i in range(j + 1):
            half, inside = divmod(place, 2 * quarter)
            part, slot = divmod(inside, quarter)
            halves[half][part, slot * BLOCK : (slot + 1) * BLOCK] = strip[
                i * BLOCK : (i + 1) * BLOCK
            ].astype(jnp.bfloat16)
            place += 1
            if place == 2 * quarter:
                send_out(0)
    squares = jnp.sum(on_diagonal, keepdims=True)
    halves[1][0, quarter * BLOCK :] = squares_tile(squares, where_ref[2])
    halves[1][1, quarter * BLOCK :] = jnp.zeros((EXTRA_ROWS, BLOCK), jnp.bfloat16)
    send_out(1)
    for copy in copies:
        copy.wait()


def gram_step(where, moved):
    columns = moved.shape[1]
    quarter = len(block_places(columns)) // 4 * BLOCK
    shapes = [(quarter, BLOCK), (quarter + EXTRA_ROWS, BLOCK)]
    return pl.pallas_call(
        gram_kernel,
        in_specs=[
            pl.BlockSpec(memory_space=pltpu.SMEM),
            pl.BlockSpec(memory_space=pltpu.VMEM),
        ],
        out_specs=[pl.BlockSpec(memory_space=pl.ANY)] * 4,
        out_shape=[jax.ShapeDtypeStruct(shapes[n // 2], jnp.bfloat16) for n in range(4)],
        scratch_shapes=[pltpu.VMEM((2, *shape), jnp.bfloat16) for shape in shapes]
        + [pltpu.SemaphoreType.DMA((4,)), pltpu.VMEM(moved.shape[::-1], jnp.bfloat16)],
        compiler_params=pltpu.CompilerParams(vmem_limit_bytes=VMEM_BYTES),
        cost_estimate=SMALL_COST,
        name="gram",
    )(where, moved)


def times_gram(left_ref, gram_ref, j):
    start = j * BLOCK
    stop = start + BLOCK
    total = lax.dot_general(
        left_ref[:, start:],
        gram_ref[start:stop, start:],
        (((1,), (1,)), ((), ())),
        preferred_element_type=jnp.float32,
    )
    if j > 0:
        total += jnp.dot(
            left_ref[:, :start], gram_ref[:start, start:stop], preferred_element_type=jnp.float32
        )
    return total


def update_kernel(slot_ref, place_ref, rows_ref, *refs):
    pieces = refs[:4]
    out_ref, gram_ref, normal_ref, product_ref = refs[-4:]
    columns = gram_ref.shape[0]
    count = columns // BLOCK
    piece_blocks = pieces[0].shape[0] // BLOCK
    squares = sum(
        jnp.sum(piece[piece_blocks * BLOCK :].astype(jnp.float32), keepdims=True)
        for piece in pieces[2:]
    )
    factor = 0.5 * math.sqrt(columns) / jnp.sqrt(squares + 1e-06)
    factor_squared = factor * factor

    @pl.when(pl.program_id(0) == 0)
    def _():
        finite = squares < math.inf
        for number, piece in enumerate(pieces):
            for block in range(piece_blocks):
                index = number * piece_blocks + block
                row = pl.multiple_of(place_ref[0, index], BLOCK)
                column = pl.multiple_of(place_ref[1, index], BLOCK)
                value = piece[block * BLOCK : (block + 1) * BLOCK]
                gram_ref[pl.ds(row, BLOCK), pl.ds(column, BLOCK)] = jnp.where(
                    finite, value, jnp.zeros_like(value)
                )

    normal_ref[...] = (rows_ref[...].astype(jnp.float32) * factor).astype(jnp.bfloat16)
    for j in range(count):
        product = times_gram(normal_ref, gram_ref, j) * factor_squared
        product_ref[:, j * BLOCK : (j + 1) * BLOCK] = product.astype(jnp.bfloat16)
    for j in range(count):
        here = slice(j * BLOCK, (j + 1) * BLOCK)
        second = times_gram(product_ref, gram_ref, j) * factor_squared
        orthogonal = (
            3.4445 * normal_ref[:, here].astype(jnp.float32)
            - 4.775 * product_ref[:, here].astype(jnp.float32)
            + 2.0315 * second
        )
        out_ref[0, :, here] = (orthogonal * math.sqrt(D)).astype(jnp.bfloat16)


def update_step(slot, places, moved, pieces, earlier=None, count=1):
    rows, columns = moved.shape
    step = rows // 2 if rows % 32 == 0 and rows >= 512 else rows
    in_specs = [pl.BlockSpec((step, columns), lambda r, *_: (r, 0))]
    in_specs += [pl.BlockSpec(piece.shape, lambda r, *_: (0, 0)) for piece in pieces]
    operands = [slot, places, moved, *pieces]
    aliases = {}
    if earlier is not None:
        in_specs.append(pl.BlockSpec(memory_space=pl.ANY))
        operands.append(earlier)
        aliases = {7: 0}
    return pl.pallas_call(
        update_kernel,
        grid_spec=pltpu.PrefetchScalarGridSpec(
            num_scalar_prefetch=2,
            grid=(rows // step,),
            in_specs=in_specs,
            out_specs=pl.BlockSpec((1, step, columns), lambda r, slot, *_: (slot[0], r, 0)),
            scratch_shapes=[
                pltpu.VMEM((columns, columns), jnp.bfloat16),
                pltpu.VMEM((step, columns), jnp.bfloat16),
                pltpu.VMEM((step, columns), jnp.bfloat16),
            ],
        ),
        out_shape=jax.ShapeDtypeStruct((count, rows, columns), jnp.bfloat16),
        input_output_aliases=aliases,
        compiler_params=pltpu.CompilerParams(vmem_limit_bytes=VMEM_BYTES),
        cost_estimate=SMALL_COST,
        name="update",
    )(*operands)


def place_kernel(cuts, slot_ref, *refs):
    for number in range(cuts):

        @pl.when(pl.program_id(0) == number)
        def _():
            refs[-1][...] = refs[number][...]


def place_step(slot, arrived, earlier, count):
    cuts = len(arrived)
    _, rows, columns = arrived[0].shape
    in_specs = [pl.BlockSpec((1, rows, columns), lambda r, slot: (0, 0, 0))] * cuts
    operands = [slot, *arrived]
    aliases = {}
    if earlier is not None:
        in_specs.append(pl.BlockSpec(memory_space=pl.ANY))
        operands.append(earlier)
        aliases = {cuts + 1: 0}
    return pl.pallas_call(
        functools.partial(place_kernel, cuts),
        grid_spec=pltpu.PrefetchScalarGridSpec(
            num_scalar_prefetch=1,
            grid=(cuts,),
            in_specs=in_specs,
            out_specs=pl.BlockSpec((1, rows, columns), lambda r, slot: (slot[0], r, 0)),
        ),
        out_shape=jax.ShapeDtypeStruct((count, cuts * rows, columns), jnp.bfloat16),
        input_output_aliases=aliases,
        compiler_params=pltpu.CompilerParams(vmem_limit_bytes=VMEM_BYTES),
        cost_estimate=SMALL_COST,
        name="place",
    )(*operands)


def add_up(mine, arrived):
    return (mine.astype(jnp.float32) + arrived.astype(jnp.float32)).astype(jnp.bfloat16)


class Routes:
    def __init__(self, dp_count):
        everyone = range(dp_count)
        line = lambda i: i >> 1 & 3
        self.side = [(i, i ^ 1) for i in everyone]
        self.inner_side = [(i, i ^ 1) for i in everyone if line(i) in (1, 2)]
        self.inward = [(i, i + 2) for i in everyone if line(i) == 0]
        self.inward += [(i, i - 2) for i in everyone if line(i) == 3]
        self.outward = [(b, a) for a, b in self.inward]
        self.middle = [(i, i + 2) for i in everyone if line(i) == 1]
        self.middle += [(i, i - 2) for i in everyone if line(i) == 2]
        self.far = []
        distance = 8
        while distance < dp_count:
            self.far.append([(i, i ^ distance) for i in everyone])
            distance *= 2


def send(value, pairs):
    return lax.ppermute(value, "dp", pairs)


class SideFirst:
    hops = {
        "side": ("side", (), 0),
        "in": ("inward", ("side",), 1),
        "middle": ("middle", ("in",), 1),
        "out": ("outward", ("middle",), 1),
        "gather": ("side", ("out",), 1),
    }

    def __init__(self, routes, place, kept, given):
        self.routes, self.inner = routes, place.inner
        self.kept, self.given = kept, given

    def value(self, hop, got):
        if hop == "side":
            return self.given
        if hop == "in":
            self.total = add_up(self.kept, got["side"])
        elif hop == "middle":
            self.total = add_up(self.total, got["in"])
        elif hop == "out":
            self.total = add_up(self.total, got["middle"])
            for pairs in self.routes.far:
                self.total = add_up(self.total, send(self.total, pairs))
        else:
            self.total = jnp.where(self.inner, self.total, got["out"])
        return self.total

    def pieces(self, got):
        return self.total, got["gather"]


class LineFirst:
    hops = {
        "in given": ("inward", (), 0),
        "in kept": ("inward", (), 0),
        "middle": ("middle", ("in given",), 1),
        "side": ("inner_side", ("in kept", "middle"), 2),
        "middle back": ("middle", ("side",), 1),
        "out": ("outward", ("side",), 0),
        "out other": ("outward", ("middle back",), 0),
    }

    def __init__(self, routes, place, kept, given):
        self.routes, self.inner = routes, place.inner
        self.kept, self.given = kept, given
        self.total = None

    def value(self, hop, got):
        if hop == "in given":
            return self.given
        if hop == "in kept":
            return self.kept
        if hop == "middle":
            return add_up(self.given, got["in given"])
        if hop == "side":
            self.kept = add_up(add_up(self.kept, got["in kept"]), got["middle"])
            return self.kept
        if hop == "out other":
            return got["middle back"]
        if self.total is None:
            self.total = add_up(self.kept, got["side"])
            for pairs in self.routes.far:
                self.total = add_up(self.total, send(self.total, pairs))
        return self.total

    def pieces(self, got):
        return (
            jnp.where(self.inner, self.total, got["out"]),
            jnp.where(self.inner, got["middle back"], got["out other"]),
        )


def plan(experts):
    transfer, latency, issue, pass_over = 23.3, 3.0, 2.5, 1.8
    takes = {"momentum": 12.0, "gram": 9.0, "update": 28.0, "place": 5.0}
    near, far = 12.0, 78.0
    deepest, patience, backlog = 4, 4.0, 10.0
    hops = {}
    for expert in range(experts):
        for kind in (LineFirst, SideFirst):
            for name, (link, needs, passes) in kind.hops.items():
                needed = [(expert, kind, need) for need in needs]
                hops[expert, kind, name] = (link.replace("inner_", ""), needed, passes)
    lengths = {}

    def length(hop):
        if hop not in lengths:
            later = [length(h) for h in hops if hop in hops[h][1]]
            lengths[hop] = 1 + max(later, default=0)
        return lengths[hop]

    def rank(hop):
        return hop[0] - length(hop) - (0.5 if hop[1] is SideFirst else 0), hop[0]

    first_choice = sorted(hops, key=rank)
    order = []
    now = 0.0
    count = dict.fromkeys(takes, 0)
    arrival = {}
    queues = {link: [] for link, _, _ in hops.values()}
    update_arrival = {}
    far_free = 0.0
    taken = set()

    def put(action, which):
        arrived = [hop for hop in arrival if arrival[hop] <= now and hop not in taken]
        taken.update(arrived)
        order.append((action, which, arrived))

    def do(kernel):
        nonlocal now
        put(kernel, count[kernel])
        count[kernel] += 1
        now += takes[kernel]

    def next_hop():
        for hop in first_choice:
            link, needed, _ = hops[hop]
            queued = sum(time > now for time in queues[link])
            if hop[0] < count["gram"] and hop not in arrival and queued < deepest:
                if all(arrival.get(need, math.inf) <= now for need in needed):
                    return hop
        return None

    do("momentum")
    do("gram")
    while count["place"] < experts - 1:
        updating = count["update"]
        last = updating == experts - 1
        early = count["place"] < experts - 3 and len(arrival) > len(hops) - 3
        early = early or updating == experts
        mine = [h for h in hops if h[0] == updating]
        whole = updating < experts and all(arrival.get(h, math.inf) <= now for h in mine)
        if updating == experts - 2:
            whole = whole and len(arrival) == len(hops)
        if last:
            whole = whole and count["place"] >= experts - 3
        coming = min((time for time in arrival.values() if time > now), default=math.inf)
        ahead = min(max([0.0] + [time - now for time in queue]) for queue in queues.values())
        free = last or coming - now >= patience or ahead >= backlog
        hop = next_hop()
        if hop is not None:
            link, _, passes = hops[hop]
            put("hop", hop)
            now += issue + passes * pass_over
            queue = queues[link]
            queue.append(max([now + 1, *queue[-1:]]) + transfer)
            arrival[hop] = queue[-1] + latency
        elif count["gram"] < count["momentum"]:
            do("gram")
        elif count["momentum"] < experts:
            do("momentum")
        elif whole and free:
            do("update")
            if updating < experts - 2:
                far_free = max(now, far_free) + far
                update_arrival[updating] = far_free
            else:
                update_arrival[updating] = now + near
        elif early and update_arrival.get(count["place"], math.inf) <= now:
            do("place")
        else:
            times = [*arrival.values(), *update_arrival.values()]
            now = min(time for time in times if time > now)
    return order


class Place:
    def __init__(self, index):
        line = index >> 1 & 3
        self.side = index & 1
        self.upper_line = line >> 1
        self.inner = (line == 1) | (line == 2)


def shards(grad, momentum, placement):
    local_count, row_count, columns = grad.shape
    group_count = lax.axis_size("expert")
    routes = Routes(lax.axis_size("dp"))
    my_group = lax.axis_index("expert")
    my_place = Place(lax.axis_index("dp"))

    slot_ids = lax.iota(jnp.int32, local_count)
    moves = placement.reshape(group_count, local_count)

    def route(group, target):
        row = lax.dynamic_index_in_dim(moves, group, keepdims=False)
        chosen = row // local_count == target
        old_slot = jnp.sum(jnp.where(chosen, slot_ids, 0))
        new_slot = jnp.sum(jnp.where(chosen, row % local_count, 0))
        return old_slot, new_slot

    places = jnp.array(block_places(columns), jnp.int32) * BLOCK
    quarter = places.shape[0] // 4
    quarters = places.reshape(4, quarter, 2)
    order = jnp.stack(
        [my_place.side, 1 - my_place.side, 2 + my_place.upper_line, 3 - my_place.upper_line]
    )
    my_places = jnp.take(quarters, order, axis=0).reshape(4 * quarter, 2).T

    where = jnp.stack([my_place.side, my_place.upper_line, lax.axis_index("dp")])

    distances = list(range(group_count - 1, -1, -1))
    momentum_new = None
    update = None
    moved, chains, got, leaving = {}, {}, {}, {}
    front = ()

    def follow(*values):
        return lax.optimization_barrier((values, front))[0]

    for action, which, arrived_hops in plan(group_count):
        taken = follow(*[got[e, kind][name] for e, kind, name in arrived_hops])
        for (e, kind, name), arrival in zip(arrived_hops, taken):
            got[e, kind][name] = arrival
        front = (*front, *taken)
        if action == "hop":
            e, kind, name = which
            needs = kind.hops[name][1]
            arrived = dict(zip(needs, follow(*[got[e, kind][need] for need in needs])))
            (value,) = follow(chains[e, kind].value(name, arrived))
            got[e, kind][name] = send(value, getattr(routes, kind.hops[name][0]))
            front = (value,)
        elif action == "momentum":
            old_slot, _ = route(my_group, my_group ^ distances[which])
            (old_slot,) = follow(old_slot.reshape(1))
            momentum_new, moved[which] = momentum_step(old_slot, grad, momentum, momentum_new)
            front = (moved[which],)
        elif action == "gram":
            (rows,) = follow(moved[which])
            parts = gram_step(where, rows)
            chains[which, SideFirst] = SideFirst(routes, my_place, *parts[:2])
            chains[which, LineFirst] = LineFirst(routes, my_place, *parts[2:])
            got[which, SideFirst], got[which, LineFirst] = {}, {}
            front = tuple(parts[3:])
        elif action == "update":
            pieces = chains[which, SideFirst].pieces(got[which, SideFirst])
            pieces += chains[which, LineFirst].pieces(got[which, LineFirst])
            pieces = follow(*pieces)
            new_slot = route(my_group ^ distances[which], my_group)[1].reshape(1)
            rows = moved[which]
            if distances[which] == 0:
                update = update_step(
                    new_slot, my_places, rows, pieces, update, local_count
                )
                front = (update,)
            else:
                here = jnp.zeros((1,), jnp.int32)
                mine = update_step(here, my_places, rows, pieces)
                pairs = [(g, g ^ distances[which]) for g in range(group_count)]
                cuts = 4 if distances[which] == 1 and row_count % 64 == 0 else 1
                cut_rows = [
                    lax.ppermute(cut, "expert", pairs) for cut in jnp.split(mine, cuts, axis=1)
                ]
                leaving[which] = new_slot, cut_rows
                front = (mine,)
        else:
            new_slot, arrived = leaving[which]
            (new_slot,) = follow(new_slot)
            update = place_step(new_slot, arrived, update, local_count)
            front = (update,)
    return momentum_new, update


def solution(mesh):
    return jax.shard_map(
        shards,
        mesh=mesh,
        in_specs=(P("expert", "dp", None), P("expert", "dp", None), P()),
        out_specs=(P("expert", "dp", None), P("expert", "dp", None)),
        check_vma=False,
    )
```
